32 devices in a mesh: groups: 2 (over x), owner: 8 (over z, y), render: 2 (over core).
Axes of the slice: x: 2, y: 2, z: 4, core: 2. Of those that a mesh axis runs over, the one named last changes fastest.
Arguments:
- params: float32 [59, 131072], P(None, ('groups', 'owner', 'render')), parts along dimension 1
- first_moment: float32 [59, 131072], P(None, ('groups', 'owner', 'render')), parts along dimension 1, may hold values from -0.012 to 0.012
- second_moment: float32 [59, 131072], P(None, ('groups', 'owner', 'render')), parts along dimension 1, may hold values from 0.0001 to 0.1
- target: float32 [3, 512, 256], P(None, ('groups', 'owner', 'render')), parts along dimension 1, may hold values from 0 to 1
- view_yaw: float32 [32], P('groups'), parts along dimension 0, may hold values from -3.1416 to 3.1416, as said below
- tile_ids: int32 [512], P(('groups', 'owner', 'render')), parts along dimension 0, may hold values from 0 to 130559, as said below
- visible: int32 [32, 16, 256], P(('groups', 'owner', 'render')), parts along dimension 0, may hold values from 0 to 4095, as said below
- tile_slots: int32 [512, 256], P(('groups', 'owner', 'render')), parts along dimension 0, may hold values from 0 to 4095, as said below
- depth_rank: int32 [512, 256], P(('groups', 'owner', 'render')), parts along dimension 0, may hold values from 0 to 255, each once within a row
Outputs:
- new_params: float32 [59, 131072], P(None, ('groups', 'owner', 'render')), parts along dimension 1
- new_first: float32 [59, 131072], P(None, ('groups', 'owner', 'render')), parts along dimension 1
- new_second: float32 [59, 131072], P(None, ('groups', 'owner', 'render')), parts along dimension 1
- rendered: float32 [3, 512, 256], P(None, ('groups', 'owner', 'render')), parts along dimension 1
The draws below stay inside these ranges and needn't reach their ends.
There are 2 independent parts, one for each index of `groups`. The reference program is written for one: setup_inputs(seed, part) draws one part's arguments, and reference() takes and returns one part's arrays. A program takes and returns all parts, laid end to end along the dimension named above; each array names one. Nothing has to cross between parts.
Inputs may be any that keep to these rules, and one draw needn't show every extreme that they name: `tile_ids`: distinct tiles of the 16 views; the 16 tiles of one device lie in one view. `view_yaw`: camera yaws, one a view. `visible`: for each device and owner, the first slots hold distinct local indices (used slots) and the rest hold 0 and are named by no list. No Gaussian is requested by two devices. Some owner gets all 256 slots used by every device, and every device uses all 256 slots for some owner. `tile_slots`: A slot o * 256 + s of the tile's device names its request visible[d, o, s]; every entry names a used slot, and every used slot of a device is named by one or two entries, in different tiles of that device. `depth_rank`: each row is a permutation.
All inputs are finite; a program needn't handle non-finite values.
Results may differ from the reference program's by a relative error of at most 0.0003.
Values sent between devices are 32-bit elements; how exact they have to be, the bound alone decides.
A program may use at most 64 MiB of HBM per device.

```python
import math
import jax
import jax.numpy as jnp
from jax import lax

NPAR = 59
PIX = 256
LIST = 256
VIEWS = 16
ADAM_STEP = 10
G_DEV = 4096
TILES_DEV = 16
OWNERS = 16
GAUSS = 65536
TILES = 256
CAP = 256


def coverage_plan(key):
    subkeys = jax.random.split(key, 7)
    lowest = max(1, (CAP + 1) // 2)
    counts = jax.random.randint(subkeys[0], (OWNERS, OWNERS), lowest, CAP + 1)
    busiest = jax.random.randint(subkeys[1], (), 0, OWNERS)
    favored = jax.random.randint(subkeys[2], (OWNERS,), 0, OWNERS)
    columns = jnp.arange(OWNERS)[None, :]
    counts = jnp.where((columns == busiest) | (columns == favored[:, None]), CAP, counts)
    shuffle = jnp.argsort(jax.random.randint(subkeys[3], (OWNERS, G_DEV), 0, 2 ** 16) * G_DEV + jnp.arange(G_DEV)[None, :], axis=1)
    starts = jax.random.randint(subkeys[4], (OWNERS,), 0, G_DEV)
    places = (starts[None, :, None] + jnp.arange(OWNERS)[:, None, None] * CAP + jnp.arange(CAP)[None, None, :]) % G_DEV
    local_rows = shuffle[jnp.arange(OWNERS)[None, :, None], places]
    used_slot = jnp.arange(CAP)[None, None, :] < counts[:, :, None]
    visible = jnp.where(used_slot, local_rows, 0).astype(jnp.int32)
    slot_total = OWNERS * CAP
    rank_score = jax.random.randint(subkeys[5], (OWNERS, slot_total), 0, 2 ** 16) * slot_total + jnp.arange(slot_total)[None, :]
    scores = jnp.where(used_slot.reshape(OWNERS, slot_total), rank_score, 2 ** 30 + jnp.arange(slot_total)[None, :])
    compact = jnp.argsort(scores, axis=1)
    live_count = jnp.sum(counts, axis=1)
    list_total = TILES_DEV * LIST
    linear = jnp.arange(LIST)[None, :] * TILES_DEV + jnp.arange(TILES_DEV)[:, None]
    ranks = linear[None, :, :] * live_count[:, None, None] // list_total
    slot_list = jnp.take_along_axis(compact, ranks.reshape(OWNERS, list_total), axis=1).reshape(TILES, LIST).astype(jnp.int32)
    block_count = VIEWS * 960 // TILES_DEV
    block_score = jax.random.randint(subkeys[6], (block_count,), 0, 2 ** 16) * block_count + jnp.arange(block_count)
    blocks = jnp.argsort(block_score)[:OWNERS]
    cells = blocks[:, None] * TILES_DEV + jnp.arange(TILES_DEV)[None, :]
    view_index = cells // 960
    remainder = cells % 960
    tile_list = (view_index * 8160 + (22 + remainder // 40) * 120 + 40 + remainder % 40).reshape(TILES).astype(jnp.int32)
    return (visible, slot_list, tile_list, shuffle, starts, compact, live_count)


def gaussian_homes(plan):
    shuffle, starts, compact, live_count, tile_list = (plan[3], plan[4], plan[5], plan[6], plan[2])
    position = jnp.argsort(shuffle, axis=1)
    offset = (position - starts[:, None]) % G_DEV
    device = jnp.minimum(offset // CAP, OWNERS - 1)
    slot_index = jnp.arange(OWNERS)[:, None] * CAP + offset % CAP
    rank_of = jnp.argsort(compact, axis=1)
    rank = rank_of[device, slot_index]
    live_here = live_count[device]
    first = (rank * (TILES_DEV * LIST) + live_here - 1) // live_here
    tile_local = first % TILES_DEV
    return tile_list[device * TILES_DEV + tile_local].reshape(GAUSS)


def view_angles(key):
    return jax.random.uniform(jax.random.fold_in(key, 11), (VIEWS,), jnp.float32, -3.14, 3.14)


def draw_visible(key, part):
    shared = coverage_plan(key)
    return shared[0]


def draw_tile_slots(key, part):
    shared = coverage_plan(key)
    return shared[1]


def draw_tile_ids(key, part):
    shared = coverage_plan(key)
    return shared[2]


def draw_view_yaw(key, part):
    return view_angles(key)


def draw_params(key, part):
    plan = coverage_plan(key)
    angles = view_angles(key)
    home = gaussian_homes(plan)
    key = jax.random.fold_in(key, 3)
    subkeys = jax.random.split(key, 3)
    shape = (NPAR, GAUSS)
    uniform_part = jax.random.uniform(subkeys[0], shape, jnp.float32, -1.0, 1.0)
    spread = jax.random.truncated_normal(subkeys[1], -2.5, 2.5, shape, jnp.float32)
    scale_low = -5.5
    scale_high = -4.2
    place = jax.random.uniform(subkeys[2], (3, GAUSS), jnp.float32, 0.0, 1.0)
    view_index = home // 8160
    within = home % 8160
    yaw = angles[view_index]
    anchor_x = (within % 120 * 16).astype(jnp.float32)
    anchor_y = (within // 120 * 16).astype(jnp.float32)
    screen_u = anchor_x + 16.0 * place[0]
    screen_v = anchor_y + 16.0 * place[1]
    depth = 3.2 + 1.6 * place[2]
    cam_x = (screen_u - 960.0) * depth / 1000.0
    cam_y = (screen_v - 540.0) * depth / 1000.0
    ahead = depth - 4.0
    cosine = jnp.cos(yaw)
    sine_yaw = jnp.sin(yaw)
    means = jnp.stack([cosine * cam_x + sine_yaw * ahead, cam_y, -sine_yaw * cam_x + cosine * ahead])
    row_index = jnp.arange(NPAR)[:, None]
    log_scale = scale_low + 0.5 * (uniform_part + 1.0) * (scale_high - scale_low)
    values = jnp.where(row_index < 6, log_scale, jnp.where(row_index < 7, 1.0 + 0.5 * uniform_part, jnp.where(row_index < 10, 0.4 * spread, jnp.where(row_index < 11, -3.5 + spread, jnp.where(row_index < 14, 0.8 * spread, 0.25 * spread)))))
    return jnp.concatenate([means, values[3:]], axis=0).astype(jnp.float32)


def block_levels(key, extent, shards, low, high):
    level = 1.0
    for dim, blocks in shards:
        heights = jax.random.uniform(jax.random.fold_in(jax.random.fold_in(key, 6), dim), (blocks,), jnp.float32, low / len(shards), high / len(shards))
        level = level * jnp.repeat(jnp.exp(heights), extent[dim] // blocks).reshape((-1,) + (1,) * (len(extent) - 1 - dim))
    return level


def centred(own_key, extent, scale, bound, cuts=(), held_as=jnp.bfloat16):
    values = scale * jax.random.normal(own_key, extent, jnp.float32)
    if cuts:
        values = values * block_levels(own_key, extent, cuts, -0.22, 0.18)
    return jnp.clip(values, -bound, bound).astype(held_as)


def setup_inputs(seed: int = 0, part: int = 0) -> dict:
    keys = jax.random.split(jax.random.key(seed), 10)
    own_keys = jax.random.split(jax.random.fold_in(keys[9], part), 10)
    params = draw_params(jax.random.fold_in(jax.random.fold_in(keys[9], part), 71), part)
    first_moment = centred(own_keys[1], (NPAR, GAUSS), 0.002, 0.012, ((1, 16),), jnp.float32)
    second_moment = jnp.clip(jnp.exp(math.log(0.1) - 6.9077553 * jax.random.uniform(own_keys[2], (NPAR, GAUSS), jnp.float32) ** block_levels(own_keys[2], (NPAR, GAUSS), ((1, 16),), -0.2, 0.2)), 0.0001, 0.1)
    target = jnp.clip(1.0 * jax.random.uniform(own_keys[3], (3, TILES, PIX), jnp.float32) ** block_levels(own_keys[3], (3, TILES, PIX), ((1, 16),), -0.2, 0.2), 0.0, 1.0)
    view_yaw = draw_view_yaw(jax.random.fold_in(jax.random.fold_in(keys[9], part), 71), part)
    tile_ids = draw_tile_ids(jax.random.fold_in(jax.random.fold_in(keys[9], part), 71), part)
    visible = draw_visible(jax.random.fold_in(jax.random.fold_in(keys[9], part), 71), part)
    tile_slots = draw_tile_slots(jax.random.fold_in(jax.random.fold_in(keys[9], part), 71), part)
    depth_rank = jax.vmap(lambda own: jax.random.permutation(own, LIST))(jax.random.split(own_keys[8], TILES)).reshape((TILES, LIST)).astype(jnp.int32)
    return {"params": params, "first_moment": first_moment, "second_moment": second_moment, "target": target, "view_yaw": view_yaw, "tile_ids": tile_ids, "visible": visible, "tile_slots": tile_slots, "depth_rank": depth_rank}


tiles_view = 8160
tiles_across = 120
focal_len = 1000.0
distance = 4.0
beta_one = 0.9
beta_two = 0.999
adam_eps = 1e-15
harm_zero = 0.28209479177387814
harm_one = 0.4886025119029199
harm_two = (1.0925484305920792, -1.0925484305920792, 0.31539156525252005, -1.0925484305920792, 0.5462742152960396)
harm_three = (-0.5900435899266435, 2.890611442640554, -0.4570457994644658, 0.3731763325901154, -0.4570457994644658, 1.445305721320277, -0.5900435899266435)

def harmonics(dir_x, dir_y, dir_z):
    sq_x = dir_x * dir_x
    sq_y = dir_y * dir_y
    sq_z = dir_z * dir_z
    terms = [jnp.full_like(dir_x, harm_zero), -harm_one * dir_y, harm_one * dir_z, -harm_one * dir_x, harm_two[0] * dir_x * dir_y, harm_two[1] * dir_y * dir_z, harm_two[2] * (2.0 * sq_z - sq_x - sq_y), harm_two[3] * dir_x * dir_z, harm_two[4] * (sq_x - sq_y), harm_three[0] * dir_y * (3.0 * sq_x - sq_y), harm_three[1] * dir_x * dir_y * dir_z, harm_three[2] * dir_y * (4.0 * sq_z - sq_x - sq_y), harm_three[3] * dir_z * (2.0 * sq_z - 3.0 * sq_x - 3.0 * sq_y), harm_three[4] * dir_x * (4.0 * sq_z - sq_x - sq_y), harm_three[5] * dir_z * (sq_x - sq_y), harm_three[6] * dir_x * (sq_x - 3.0 * sq_y)]
    return jnp.stack(terms)

def quadratic(left_vec, covariance, right_vec):
    result = 0.0
    for first in range(3):
        for second in range(3):
            result = result + left_vec[first] * covariance[first][second] * right_vec[second]
    return result

def render_tiles(slot_rows, ordered, tile_ids, view_yaw):
    entries = slot_rows[:, ordered]
    view_index = tile_ids // tiles_view
    within = tile_ids % tiles_view
    anchor_x = (within % tiles_across * 16).astype(jnp.float32)
    anchor_y = (within // tiles_across * 16).astype(jnp.float32)
    onehot = (view_index[:, None] == jnp.arange(view_yaw.shape[0], dtype=jnp.int32)[None, :]).astype(jnp.float32)
    yaw_tile = jnp.dot(onehot, view_yaw.astype(jnp.float32), precision=lax.Precision.HIGHEST)[:, None]
    cosine = jnp.cos(yaw_tile)
    sine_yaw = jnp.sin(yaw_tile)
    pos_x, pos_y, pos_z = (entries[0], entries[1], entries[2])
    cam_x = cosine * pos_x - sine_yaw * pos_z
    cam_y = pos_y
    cam_z = sine_yaw * pos_x + cosine * pos_z + distance
    inverse_z = 1.0 / cam_z
    center_u = focal_len * cam_x * inverse_z + 960.0
    center_v = focal_len * cam_y * inverse_z + 540.0
    stretch = jnp.exp(entries[3:6])
    quaternion = entries[6:10]
    quaternion = quaternion / jnp.sqrt(lax.optimization_barrier(jnp.sum(quaternion * quaternion, axis=0)))
    quat_w, quat_x, quat_y, quat_z = (quaternion[0], quaternion[1], quaternion[2], quaternion[3])
    rotation = [[1.0 - 2.0 * (quat_y * quat_y + quat_z * quat_z), 2.0 * (quat_x * quat_y - quat_w * quat_z), 2.0 * (quat_x * quat_z + quat_w * quat_y)], [2.0 * (quat_x * quat_y + quat_w * quat_z), 1.0 - 2.0 * (quat_x * quat_x + quat_z * quat_z), 2.0 * (quat_y * quat_z - quat_w * quat_x)], [2.0 * (quat_x * quat_z - quat_w * quat_y), 2.0 * (quat_y * quat_z + quat_w * quat_x), 1.0 - 2.0 * (quat_x * quat_x + quat_y * quat_y)]]
    scaled = [[rotation[first][inner] * stretch[inner] for inner in range(3)] for first in range(3)]
    covariance = [[scaled[first][0] * scaled[second][0] + scaled[first][1] * scaled[second][1] + scaled[first][2] * scaled[second][2] for second in range(3)] for first in range(3)]
    focal_z = focal_len * inverse_z
    slope_x = focal_len * cam_x * inverse_z * inverse_z
    slope_y = focal_len * cam_y * inverse_z * inverse_z
    zeros_entry = jnp.zeros_like(focal_z)
    proj_u = [focal_z * cosine - slope_x * sine_yaw, zeros_entry, -focal_z * sine_yaw - slope_x * cosine]
    proj_v = [-slope_y * sine_yaw, focal_z, -slope_y * cosine]
    cov_a = quadratic(proj_u, covariance, proj_u) + 0.3
    cov_b = quadratic(proj_u, covariance, proj_v)
    cov_c = quadratic(proj_v, covariance, proj_v) + 0.3
    determinant = cov_a * cov_c - cov_b * cov_b
    conic_a = cov_c / determinant
    conic_b = -cov_b / determinant
    conic_c = cov_a / determinant
    opacity = jax.nn.sigmoid(entries[10])
    dir_x = pos_x + distance * sine_yaw
    dir_y = pos_y
    dir_z = pos_z + distance * cosine
    length = jnp.sqrt(dir_x * dir_x + dir_y * dir_y + dir_z * dir_z)
    basis_set = harmonics(dir_x / length, dir_y / length, dir_z / length)
    coeffs = entries[11:].reshape(16, 3, entries.shape[1], entries.shape[2])
    colour = jax.nn.relu(lax.optimization_barrier(jnp.sum(basis_set[:, None] * coeffs, axis=0)) + 0.5)
    pixel_ids = jnp.arange(PIX, dtype=jnp.int32)
    pixel_x = anchor_x[:, None] + (pixel_ids % 16).astype(jnp.float32)[None, :] + 0.5
    pixel_y = anchor_y[:, None] + (pixel_ids // 16).astype(jnp.float32)[None, :] + 0.5
    delta_x = pixel_x[:, :, None] - center_u[:, None, :]
    delta_y = pixel_y[:, :, None] - center_v[:, None, :]
    exponent = -0.5 * (conic_a[:, None, :] * delta_x * delta_x + 2.0 * conic_b[:, None, :] * delta_x * delta_y + conic_c[:, None, :] * delta_y * delta_y)
    alphas = opacity[:, None, :] * jnp.exp(exponent)
    log_keep = jnp.log(1.0 - alphas)
    list_len = entries.shape[2]
    list_ids = jnp.arange(list_len, dtype=jnp.int32)
    upper_ones = (list_ids[:, None] < list_ids[None, :]).astype(jnp.float32)
    transmit = jnp.exp(jnp.einsum('tpj,jk->tpk', log_keep, upper_ones, precision=lax.Precision.HIGHEST))
    weight = alphas * transmit
    return jnp.einsum('tpl,ctl->ctp', weight, colour, precision=lax.Precision.HIGHEST)

def step_rates():
    row_index = jnp.arange(NPAR, dtype=jnp.int32)[:, None]
    rates = jnp.where(row_index < 3, 0.00016, jnp.where(row_index < 6, 0.005, jnp.where(row_index < 10, 0.001, jnp.where(row_index < 11, 0.05, jnp.where(row_index < 14, 0.0025, 0.000125)))))
    return rates.astype(jnp.float32)

def adam_update(params, moment, variance, gradient):
    moment = beta_one * moment + (1.0 - beta_one) * gradient
    variance = beta_two * variance + (1.0 - beta_two) * gradient * gradient
    fix_one = 1.0 - beta_one ** ADAM_STEP
    fix_two = 1.0 - beta_two ** ADAM_STEP
    params = params - step_rates() * (moment / fix_one) / (jnp.sqrt(variance / fix_two) + adam_eps)
    return (params, moment, variance)

def reference(params, first_moment, second_moment, target, view_yaw, tile_ids, visible, tile_slots, depth_rank):
    global_rows = (jnp.arange(OWNERS, dtype=jnp.int32)[None, :, None] * G_DEV + visible).reshape(OWNERS, OWNERS * CAP).astype(jnp.int32)
    ordered = jnp.take_along_axis(tile_slots, depth_rank, axis=1).reshape(OWNERS, TILES_DEV, LIST)
    tiles_each = tile_ids.reshape(OWNERS, TILES_DEV)
    targets = target.astype(jnp.float32).reshape(3, OWNERS, TILES_DEV, PIX).transpose(1, 0, 2, 3)
    loss_scale = 1.0 / PIX

    def visit(grad_total, inputs):
        rows_index, order_here, tiles_here, target_here = inputs
        slot_rows = params[:, rows_index]
        picture, pullback = jax.vjp(lambda values: render_tiles(values, order_here, tiles_here, view_yaw), slot_rows)
        grad_rows, = pullback((picture - target_here) * loss_scale)
        return (grad_total.at[:, rows_index].add(grad_rows.astype(grad_total.dtype)), picture)
    grad_total, pictures = lax.scan(visit, jnp.zeros((NPAR, GAUSS), jnp.float32), (global_rows, ordered, tiles_each, targets))
    rendered = pictures.transpose(1, 0, 2, 3).reshape(3, TILES, PIX)
    new_params, new_first, new_second = adam_update(params, first_moment, second_moment, grad_total)
    return (new_params, new_first, new_second, rendered)
```

```python
import functools

import jax
import jax.numpy as jnp
from jax import lax
from jax.experimental import pallas as pl
from jax.experimental.pallas import tpu as pltpu
from jax.sharding import PartitionSpec as P

NPAR = 59
PIX = 256
ADAM_STEP = 10
LANES = 128
QUANT = 9
SPLITS = 3

tiles_view = 8160
tiles_across = 120
focal_len = 1000.0
distance = 4.0
beta_one = 0.9
beta_two = 0.999
adam_eps = 1e-15
harm_zero = 0.28209479177387814
harm_one = 0.4886025119029199
harm_two = (
    1.0925484305920792,
    -1.0925484305920792,
    0.31539156525252005,
    -1.0925484305920792,
    0.5462742152960396,
)
harm_three = (
    -0.5900435899266435,
    2.890611442640554,
    -0.4570457994644658,
    0.3731763325901154,
    -0.4570457994644658,
    1.445305721320277,
    -0.5900435899266435,
)
VMEM = pltpu.CompilerParams(vmem_limit_bytes=56 * 1024 * 1024)
NN = (((1,), (0,)), ((), ()))
NT = (((1,), (1,)), ((), ()))


def mxu(left, right, dims=NN):
    return lax.dot_general(left, right, dims, preferred_element_type=jnp.float32)


def split_two(value):
    high = value.astype(jnp.bfloat16)
    low = (value - high.astype(jnp.float32)).astype(jnp.bfloat16)
    return high, low


def split_three(value):
    high = value.astype(jnp.bfloat16).astype(jnp.float32)
    rest = value - high
    mid = rest.astype(jnp.bfloat16).astype(jnp.float32)
    low = (rest - mid).astype(jnp.bfloat16).astype(jnp.float32)
    return high, mid, low


def harmonics(dir_x, dir_y, dir_z):
    sq_x = dir_x * dir_x
    sq_y = dir_y * dir_y
    sq_z = dir_z * dir_z
    return [
        jnp.full_like(dir_x, harm_zero),
        -harm_one * dir_y,
        harm_one * dir_z,
        -harm_one * dir_x,
        harm_two[0] * dir_x * dir_y,
        harm_two[1] * dir_y * dir_z,
        harm_two[2] * (2.0 * sq_z - sq_x - sq_y),
        harm_two[3] * dir_x * dir_z,
        harm_two[4] * (sq_x - sq_y),
        harm_three[0] * dir_y * (3.0 * sq_x - sq_y),
        harm_three[1] * dir_x * dir_y * dir_z,
        harm_three[2] * dir_y * (4.0 * sq_z - sq_x - sq_y),
        harm_three[3] * dir_z * (2.0 * sq_z - 3.0 * sq_x - 3.0 * sq_y),
        harm_three[4] * dir_x * (4.0 * sq_z - sq_x - sq_y),
        harm_three[5] * dir_z * (sq_x - sq_y),
        harm_three[6] * dir_x * (sq_x - 3.0 * sq_y),
    ]


def project(entries, cosine, sine_yaw):
    pos_x, pos_y, pos_z = entries[0], entries[1], entries[2]
    cam_x = cosine * pos_x - sine_yaw * pos_z
    cam_z = sine_yaw * pos_x + cosine * pos_z + distance
    inverse_z = 1.0 / cam_z
    center_u = focal_len * cam_x * inverse_z + 960.0
    center_v = focal_len * pos_y * inverse_z + 540.0
    stretch = [jnp.exp(entries[3 + axis]) for axis in range(3)]
    norm = entries[6] * entries[6] + entries[7] * entries[7]
    norm = norm + entries[8] * entries[8] + entries[9] * entries[9]
    inverse_norm = 1.0 / jnp.sqrt(norm)
    quat_w, quat_x, quat_y, quat_z = (entries[6 + part] * inverse_norm for part in range(4))
    rotation = [
        [
            1.0 - 2.0 * (quat_y * quat_y + quat_z * quat_z),
            2.0 * (quat_x * quat_y - quat_w * quat_z),
            2.0 * (quat_x * quat_z + quat_w * quat_y),
        ],
        [
            2.0 * (quat_x * quat_y + quat_w * quat_z),
            1.0 - 2.0 * (quat_x * quat_x + quat_z * quat_z),
            2.0 * (quat_y * quat_z - quat_w * quat_x),
        ],
        [
            2.0 * (quat_x * quat_z - quat_w * quat_y),
            2.0 * (quat_y * quat_z + quat_w * quat_x),
            1.0 - 2.0 * (quat_x * quat_x + quat_y * quat_y),
        ],
    ]
    focal_z = focal_len * inverse_z
    slope_x = focal_len * cam_x * inverse_z * inverse_z
    slope_y = focal_len * pos_y * inverse_z * inverse_z
    proj_u = [focal_z * cosine - slope_x * sine_yaw, None, -focal_z * sine_yaw - slope_x * cosine]
    proj_v = [-slope_y * sine_yaw, focal_z, -slope_y * cosine]
    left = [
        (proj_u[0] * rotation[0][axis] + proj_u[2] * rotation[2][axis]) * stretch[axis]
        for axis in range(3)
    ]
    right = [
        (
            proj_v[0] * rotation[0][axis]
            + proj_v[1] * rotation[1][axis]
            + proj_v[2] * rotation[2][axis]
        )
        * stretch[axis]
        for axis in range(3)
    ]
    cov_a = left[0] * left[0] + left[1] * left[1] + left[2] * left[2] + 0.3
    cov_b = left[0] * right[0] + left[1] * right[1] + left[2] * right[2]
    cov_c = right[0] * right[0] + right[1] * right[1] + right[2] * right[2] + 0.3
    determinant = cov_a * cov_c - cov_b * cov_b
    inverse_det = 1.0 / determinant
    conic_a = cov_c * inverse_det
    conic_b = -cov_b * inverse_det
    conic_c = cov_a * inverse_det
    logit = entries[10]
    tiny = logit < -80.0
    safe = jnp.where(tiny, 0.0, logit)
    log_opacity = jnp.where(tiny, logit, -jnp.log(1.0 + jnp.exp(-safe)))
    dir_x = pos_x + distance * sine_yaw
    dir_z = pos_z + distance * cosine
    inverse_len = 1.0 / jnp.sqrt(dir_x * dir_x + pos_y * pos_y + dir_z * dir_z)
    basis_set = harmonics(dir_x * inverse_len, pos_y * inverse_len, dir_z * inverse_len)
    colours = []
    for channel in range(3):
        total = basis_set[0] * entries[11 + channel]
        for term in range(1, 16):
            total = total + basis_set[term] * entries[11 + 3 * term + channel]
        total = total + 0.5
        colours.append(jnp.where(total > 0.0, total, 0.0))
    return [center_u, center_v, conic_a, conic_b, conic_c, log_opacity] + colours


def gather_columns(index, table_eight, table_one, chunks):
    low = index & (LANES - 1)
    high = lax.shift_right_logical(index, 7)
    eight = jnp.zeros((8, LANES), jnp.float32)
    one = jnp.zeros((8, LANES), jnp.float32)
    for chunk in range(chunks):
        here = high == chunk
        eight = jnp.where(here, lane_take(table_eight(chunk), low), eight)
        one = jnp.where(here, lane_take(table_one(chunk), low), one)
    return eight, one[0:1]


def lane_take(values, index):
    return jnp.take_along_axis(values, index, axis=1, mode="promise_in_bounds")


def scatter_columns(values, index, rows, total_ref):
    count = index.shape[1]
    low = index & (LANES - 1)
    high = lax.shift_right_logical(index, 7)
    low_hot = (lax.broadcasted_iota(jnp.int32, (LANES, count), 0) == low).astype(jnp.float32)
    low_hot = low_hot.astype(jnp.bfloat16)
    high_hot = lax.broadcasted_iota(jnp.int32, (rows, count), 0) == high
    for quantity in range(QUANT):
        pieces = [jnp.where(high_hot, part, 0.0) for part in split_three(values[quantity])]
        left = jnp.concatenate(pieces, axis=0).astype(jnp.bfloat16)
        sums = mxu(left, low_hot, NT)
        total_ref[pl.ds(quantity * rows, rows), :] += (
            sums[0:rows] + sums[rows : 2 * rows] + sums[2 * rows :]
        )


def load_entries(params_ref, scr, rows):
    chunks = params_ref.shape[1] // LANES
    for chunk in range(chunks):
        scr[pl.ds(chunk, NPAR, stride=rows), :] = params_ref[:, chunk * LANES : (chunk + 1) * LANES]
    scr[pl.ds(chunks, NPAR, stride=rows), :] = jnp.broadcast_to(params_ref[:, 0:1], (NPAR, LANES))
    return [scr[pl.ds(row * rows, rows), :] for row in range(NPAR)]


def owner_kernel(cap, rows, params_ref, column_ref, trig_ref, eight_ref, one_ref, yaw_ref, scr, table):
    slots = column_ref.shape[1]
    chunks = params_ref.shape[1] // LANES
    for row in range(NPAR):
        scr[pl.ds(row * rows, rows), :] = jnp.ones((rows, LANES), jnp.float32)
    column = column_ref[...]
    low_hot = lax.broadcasted_iota(jnp.int32, (LANES, slots), 0) == (column & (LANES - 1))
    high_hot = lax.broadcasted_iota(jnp.int32, (rows, slots), 0) == lax.shift_right_logical(column, 7)
    asker = (lax.broadcasted_iota(jnp.int32, (1, slots), 1) // cap).astype(jnp.float32)
    who = mxu(
        jnp.where(high_hot, asker, 0.0).astype(jnp.bfloat16),
        low_hot.astype(jnp.float32).astype(jnp.bfloat16),
        NT,
    ).astype(jnp.int32)
    row_ids = lax.broadcasted_iota(jnp.int32, (rows, LANES), 0)
    lane_ids = lax.broadcasted_iota(jnp.int32, (rows, LANES), 1)
    who = jnp.where(row_ids == chunks, lane_ids, who) & (LANES - 1)
    for part in range(2):
        known = jnp.broadcast_to(trig_ref[part : part + 1, :], (8, LANES))
        for block in range(rows // 8):
            yaw_ref[part, block * 8 : block * 8 + 8, :] = lane_take(
                known, who[block * 8 : block * 8 + 8]
            )
    entries = load_entries(params_ref, scr, rows)
    for quantity, value in enumerate(project(entries, yaw_ref[0], yaw_ref[1])):
        table[pl.ds(quantity * rows, rows), :] = value

    def table_eight(chunk):
        return table[pl.ds(chunk, 8, stride=rows), :]

    def table_one(chunk):
        return jnp.broadcast_to(table[pl.ds(8 * rows + chunk, 1), :], (8, LANES))

    @pl.loop(0, slots // LANES)
    def _(part):
        place = pl.ds(pl.multiple_of(part * LANES, LANES), LANES)
        index = jnp.broadcast_to(column_ref[:, place], (8, LANES))
        eight, one = gather_columns(index, table_eight, table_one, chunks + 1)
        eight_ref[:, place] = eight
        one_ref[:, place] = one


def tile_kernel(
    eight_ref,
    one_ref,
    slots_ref,
    rank_ref,
    anchor_ref,
    target_ref,
    out_ref,
    grad_eight_ref,
    grad_one_ref,
    total,
    weight_ref,
    ratio_ref,
    weight_high,
    weight_low,
    moment_high,
    moment_low,
):
    tiles, length = slots_ref.shape
    slots = eight_ref.shape[1]
    chunks = slots // LANES
    rows = chunks
    total[...] = jnp.zeros_like(total)
    def basis(shape, pixel_axis):
        pixel = lax.broadcasted_iota(jnp.int32, shape, pixel_axis)
        term = lax.broadcasted_iota(jnp.int32, shape, 1 - pixel_axis)
        px = (pixel & 15).astype(jnp.float32) - 7.5
        py = lax.shift_right_logical(pixel, 4).astype(jnp.float32) - 7.5
        kind = jnp.where(term < 24, term & 7, 7)
        value = jnp.where(kind == 0, 1.0, 0.0)
        value = jnp.where(kind == 1, px, value)
        value = jnp.where(kind == 2, py, value)
        value = jnp.where(kind == 3, px * px, value)
        value = jnp.where(kind == 4, px * py, value)
        value = jnp.where(kind == 5, py * py, value)
        return value.astype(jnp.bfloat16)

    basis_pixels = basis((PIX, 32), 0)
    basis_terms = basis((8, PIX), 1)
    from_ids = lax.broadcasted_iota(jnp.int32, (length, length), 0)
    to_ids = lax.broadcasted_iota(jnp.int32, (length, length), 1)
    before = (from_ids < to_ids).astype(jnp.float32).astype(jnp.bfloat16)
    after = (from_ids > to_ids).astype(jnp.float32).astype(jnp.bfloat16)

    def table_eight(chunk):
        return eight_ref[:, chunk * LANES : (chunk + 1) * LANES]

    def table_one(chunk):
        return jnp.broadcast_to(one_ref[:, chunk * LANES : (chunk + 1) * LANES], (8, LANES))

    step = 64

    @pl.loop(0, tiles)
    def _(tile):
        named = jnp.broadcast_to(slots_ref[pl.ds(tile, 1), :], (8, length))
        rank = jnp.broadcast_to(rank_ref[pl.ds(tile, 1), :], (8, length))
        halves = length // LANES
        ordered, eights, ones = [], [], []
        for half in range(halves):
            place = rank[:, half * LANES : (half + 1) * LANES]
            low = place & (LANES - 1)
            index = lane_take(named[:, 0:LANES], low)
            for other in range(1, halves):
                chosen = lane_take(named[:, other * LANES : (other + 1) * LANES], low)
                index = jnp.where(lax.shift_right_logical(place, 7) == other, chosen, index)
            eight, one = gather_columns(index, table_eight, table_one, chunks)
            ordered.append(index[0:1])
            eights.append(eight)
            ones.append(one)
        ordered = jnp.concatenate(ordered, axis=1)
        eight = jnp.concatenate(eights, axis=1)
        one = jnp.concatenate(ones, axis=1)
        off_u = eight[0:1] - anchor_ref[0, tile]
        off_v = eight[1:2] - anchor_ref[1, tile]
        con_a, con_b, con_c = eight[2:3], eight[3:4], eight[4:5]
        lin_x = con_a * off_u + con_b * off_v
        lin_y = con_b * off_u + con_c * off_v
        flat = eight[5:6] - 0.5 * (con_a * off_u * off_u + 2.0 * con_b * off_u * off_v + con_c * off_v * off_v)
        zero_row = jnp.zeros((1, length), jnp.float32)
        coefs = jnp.concatenate(
            [flat, lin_x, lin_y, -0.5 * con_a, -con_b, -0.5 * con_c, zero_row, zero_row], axis=0
        )
        zero_eight = jnp.zeros((8, length), jnp.float32)
        coefs = jnp.concatenate(list(split_three(coefs)) + [zero_eight], axis=0).astype(jnp.bfloat16)
        for part in range(PIX // step):
            span = slice(part * step, (part + 1) * step)
            alpha = jnp.exp(mxu(basis_pixels[span], coefs))
            keep = 1.0 - alpha
            high, low = split_two(jnp.log(keep))
            transmit = jnp.exp(mxu(high, before) + mxu(low, before))
            weight = alpha * transmit
            weight_ref[span, :] = weight
            ratio_ref[span, :] = alpha / keep
            high, low = split_two(weight)
            weight_high[span, :] = high
            weight_low[span, :] = low
        colour = jnp.concatenate([eight[6:8], one] + [zero_row] * 5, axis=0)
        col_h, col_m, col_l = split_three(colour)
        col_stack = jnp.concatenate([col_h, col_m, col_l, zero_eight], axis=0).astype(jnp.bfloat16)
        from_high = mxu(col_stack, weight_high[...], NT)
        from_low = mxu(col_stack, weight_low[...], NT)
        image = from_high[0:8] + (from_high[8:16] + from_low[0:8])
        image = image + (from_high[16:24] + from_low[8:16])
        wanted = []
        for channel in range(3):
            out_ref[channel, pl.ds(tile, 1), :] = image[channel : channel + 1]
            wanted.append(target_ref[channel, pl.ds(tile, 1), :])
        zero_pix = jnp.zeros((1, PIX), jnp.float32)
        wanted = jnp.concatenate(wanted + [zero_pix] * 5, axis=0)
        gradient = (image - wanted) * (1.0 / PIX)
        gr_h, gr_m, gr_l = split_three(gradient)
        zero_more = jnp.zeros((80, PIX), jnp.float32)
        gr_stack = jnp.concatenate([gr_h, gr_h, gr_h, gr_m, gr_m, gr_l, zero_more], axis=0)
        gr_turned = gr_stack.T.astype(jnp.bfloat16)
        zero_more = jnp.zeros((80, length), jnp.float32)
        col_all = jnp.concatenate([col_h, col_m, col_l, col_h, col_m, col_h, zero_more], axis=0)
        col_all = col_all.astype(jnp.bfloat16)
        for part in range(PIX // step):
            span = slice(part * step, (part + 1) * step)
            pull = mxu(gr_turned[span], col_all) * weight_ref[span, :]
            high, low = split_two(pull)
            behind = mxu(high, after) + mxu(low, after)
            high, low = split_two(pull - behind * ratio_ref[span, :])
            moment_high[span, :] = high
            moment_low[span, :] = low
        moments = mxu(basis_terms, moment_high[...]) + mxu(basis_terms, moment_low[...])
        gr_stack = jnp.concatenate([gr_h, gr_m, gr_l, jnp.zeros((8, PIX), jnp.float32)], axis=0)
        gr_stack = gr_stack.astype(jnp.bfloat16)
        from_high = mxu(gr_stack, weight_high[...])
        from_low = mxu(gr_stack, weight_low[...])
        d_colour = from_high[0:8] + (from_high[8:16] + from_low[0:8])
        d_colour = d_colour + (from_high[16:24] + from_low[8:16])
        m_0, m_x, m_y = moments[0:1], moments[1:2], moments[2:3]
        m_xx, m_xy, m_yy = moments[3:4], moments[4:5], moments[5:6]
        shift_x = m_x - off_u * m_0
        shift_y = m_y - off_v * m_0
        values = [
            con_a * shift_x + con_b * shift_y,
            con_b * shift_x + con_c * shift_y,
            -0.5 * (m_xx - off_u * (m_x + shift_x)),
            -(m_xy - off_u * m_y - off_v * shift_x),
            -0.5 * (m_yy - off_v * (m_y + shift_y)),
            m_0,
            d_colour[0:1],
            d_colour[1:2],
            d_colour[2:3],
        ]
        scatter_columns(values, ordered, rows, total)

    for chunk in range(chunks):
        grad_eight_ref[:, chunk * LANES : (chunk + 1) * LANES] = total[pl.ds(chunk, 8, stride=rows), :]
        grad_one_ref[:, chunk * LANES : (chunk + 1) * LANES] = total[pl.ds(8 * rows + chunk, 1), :]


def update_kernel(
    rows,
    params_ref,
    first_ref,
    second_ref,
    column_ref,
    yaw_ref,
    eight_ref,
    one_ref,
    new_params_ref,
    new_first_ref,
    new_second_ref,
    scr,
    total,
):
    slots = column_ref.shape[1]
    chunks = params_ref.shape[1] // LANES
    for row in range(NPAR):
        scr[pl.ds(row * rows, rows), :] = jnp.ones((rows, LANES), jnp.float32)
    total[...] = jnp.zeros_like(total)
    width = 256

    @pl.loop(0, slots // width)
    def _(part):
        place = pl.ds(pl.multiple_of(part * width, width), width)
        values = [eight_ref[pl.ds(row, 1), place] for row in range(8)] + [one_ref[:, place]]
        scatter_columns(values, column_ref[:, place], rows, total)

    entries = load_entries(params_ref, scr, rows)
    pulls = [total[pl.ds(quantity * rows, rows), :] for quantity in range(QUANT)]
    size = jnp.abs(pulls[0])
    for pull in pulls[1:]:
        size = jnp.maximum(size, jnp.abs(pull))
    touched = size > 0.0
    _, pullback = jax.vjp(lambda values: project(values, yaw_ref[0], yaw_ref[1]), entries)
    (gradients,) = pullback(pulls)
    for row in range(NPAR):
        scr[pl.ds(row * rows, rows), :] = jnp.where(touched, gradients[row], 0.0)
    extra = jnp.sum(scr[pl.ds(chunks, NPAR, stride=rows), :], axis=1, keepdims=True)
    lane = lax.broadcasted_iota(jnp.int32, (NPAR, LANES), 1)
    row_index = lax.broadcasted_iota(jnp.int32, (NPAR, LANES), 0)
    rates = jnp.where(row_index < 14, 0.0025, 0.000125)
    rates = jnp.where(row_index < 11, 0.05, rates)
    rates = jnp.where(row_index < 10, 0.001, rates)
    rates = jnp.where(row_index < 6, 0.005, rates)
    rates = jnp.where(row_index < 3, 0.00016, rates)
    fix_one = 1.0 - beta_one**ADAM_STEP
    fix_two = 1.0 - beta_two**ADAM_STEP
    for chunk in range(chunks):
        place = slice(chunk * LANES, (chunk + 1) * LANES)
        gradient = scr[pl.ds(chunk, NPAR, stride=rows), :]
        if chunk == 0:
            gradient = gradient + jnp.where(lane == 0, extra, 0.0)
        moment = beta_one * first_ref[:, place] + (1.0 - beta_one) * gradient
        variance = beta_two * second_ref[:, place] + (1.0 - beta_two) * gradient * gradient
        change = rates * (moment / fix_one) / (jnp.sqrt(variance / fix_two) + adam_eps)
        new_params_ref[:, place] = params_ref[:, place] - change
        new_first_ref[:, place] = moment
        new_second_ref[:, place] = variance


def exchange(values, owners, cap):
    rows = values.shape[0]
    sent = values.reshape(rows, owners, cap)
    got = lax.all_to_all(sent, ("owner", "render"), split_axis=1, concat_axis=1, tiled=True)
    return got.reshape(rows, owners * cap)


def body(
    params, first_moment, second_moment, target, view_yaw, tile_ids, visible, tile_slots, depth_rank
):
    owners = lax.axis_size(("owner", "render"))
    cap = visible.shape[2]
    slots = owners * cap
    held = params.shape[1]
    tiles, length = tile_slots.shape
    chunks = held // LANES
    rows = (chunks + 1 + 7) // 8 * 8
    f32 = jnp.float32
    view = tile_ids[0] // tiles_view
    requests = jnp.concatenate(
        [visible[0], jnp.full((owners, 1), view, jnp.int32)], axis=1
    )
    wanted = lax.all_to_all(requests, ("owner", "render"), split_axis=0, concat_axis=0, tiled=True)
    index = wanted[:, :cap]
    asker = jnp.arange(owners, dtype=jnp.int32)[:, None]
    column = jnp.where(index == 0, held + asker, index).reshape(1, slots)
    view_ids = jnp.arange(view_yaw.shape[0], dtype=jnp.int32)
    yaw = jnp.sum(jnp.where(wanted[:, cap][:, None] == view_ids[None, :], view_yaw[None, :], 0.0), axis=1)
    trig = jnp.stack([jnp.cos(yaw), jnp.sin(yaw)])
    trig = jnp.pad(trig, ((0, 6), (0, LANES - owners)))
    eight, one, yaws = pl.pallas_call(
        functools.partial(owner_kernel, cap, rows),
        out_shape=[
            jax.ShapeDtypeStruct((8, slots), f32),
            jax.ShapeDtypeStruct((1, slots), f32),
            jax.ShapeDtypeStruct((2, rows, LANES), f32),
        ],
        scratch_shapes=[pltpu.VMEM((NPAR * rows, LANES), f32), pltpu.VMEM((QUANT * rows, LANES), f32)],
        compiler_params=VMEM,
        name="owner_project",
    )(params, column, trig)
    both = exchange(jnp.concatenate([eight, one], axis=0), owners, cap)
    within = tile_ids % tiles_view
    anchors = jnp.stack([within % tiles_across, within // tiles_across]).astype(f32) * 16.0 + 8.0
    vmem = pl.BlockSpec(memory_space=pltpu.VMEM)
    rendered, grad_eight, grad_one = pl.pallas_call(
        tile_kernel,
        out_shape=[
            jax.ShapeDtypeStruct(target.shape, f32),
            jax.ShapeDtypeStruct((8, slots), f32),
            jax.ShapeDtypeStruct((1, slots), f32),
        ],
        in_specs=[vmem, vmem, vmem, vmem, pl.BlockSpec(memory_space=pltpu.SMEM), vmem],
        scratch_shapes=[
            pltpu.VMEM((QUANT * slots // LANES, LANES), f32),
            pltpu.VMEM((PIX, length), f32),
            pltpu.VMEM((PIX, length), f32),
            pltpu.VMEM((PIX, length), jnp.bfloat16),
            pltpu.VMEM((PIX, length), jnp.bfloat16),
            pltpu.VMEM((PIX, length), jnp.bfloat16),
            pltpu.VMEM((PIX, length), jnp.bfloat16),
        ],
        compiler_params=VMEM,
        name="tile_step",
    )(both[:8], both[8:], tile_slots, depth_rank, anchors, target)
    back = exchange(jnp.concatenate([grad_eight, grad_one], axis=0), owners, cap)
    new_params, new_first, new_second = pl.pallas_call(
        functools.partial(update_kernel, rows),
        out_shape=[jax.ShapeDtypeStruct(params.shape, f32)] * 3,
        scratch_shapes=[pltpu.VMEM((NPAR * rows, LANES), f32), pltpu.VMEM((QUANT * rows, LANES), f32)],
        compiler_params=VMEM,
        name="adam_step",
    )(params, first_moment, second_moment, column, yaws, back[:8], back[8:])
    return (new_params, new_first, new_second, rendered)


def solution(mesh):
    in_specs = (
        P(None, ("groups", "owner", "render")),
        P(None, ("groups", "owner", "render")),
        P(None, ("groups", "owner", "render")),
        P(None, ("groups", "owner", "render"), None),
        P("groups"),
        P(("groups", "owner", "render")),
        P(("groups", "owner", "render"), None, None),
        P(("groups", "owner", "render"), None),
        P(("groups", "owner", "render"), None),
    )
    out_specs = (
        P(None, ("groups", "owner", "render")),
        P(None, ("groups", "owner", "render")),
        P(None, ("groups", "owner", "render")),
        P(None, ("groups", "owner", "render"), None),
    )
    return jax.shard_map(body, mesh=mesh, in_specs=in_specs, out_specs=out_specs, check_vma=False)
```

```python
import functools

import jax
import jax.numpy as jnp
from jax import lax
from jax.experimental import pallas as pl
from jax.experimental.pallas import tpu as pltpu
from jax.sharding import PartitionSpec as P

NPAR = 59
PIX = 256
ADAM_STEP = 10
LANES = 128
QUANT = 9
SPLITS = 3

tiles_view = 8160
tiles_across = 120
focal_len = 1000.0
distance = 4.0
beta_one = 0.9
beta_two = 0.999
adam_eps = 1e-15
harm_zero = 0.28209479177387814
harm_one = 0.4886025119029199
harm_two = (
    1.0925484305920792,
    -1.0925484305920792,
    0.31539156525252005,
    -1.0925484305920792,
    0.5462742152960396,
)
harm_three = (
    -0.5900435899266435,
    2.890611442640554,
    -0.4570457994644658,
    0.3731763325901154,
    -0.4570457994644658,
    1.445305721320277,
    -0.5900435899266435,
)
VMEM = pltpu.CompilerParams(vmem_limit_bytes=56 * 1024 * 1024)
NN = (((1,), (0,)), ((), ()))
NT = (((1,), (1,)), ((), ()))


def mxu(left, right, dims=NN):
    return lax.dot_general(left, right, dims, preferred_element_type=jnp.float32)


def split_two(value):
    high = value.astype(jnp.bfloat16)
    low = (value - high.astype(jnp.float32)).astype(jnp.bfloat16)
    return high, low


def split_three(value):
    high = value.astype(jnp.bfloat16).astype(jnp.float32)
    rest = value - high
    mid = rest.astype(jnp.bfloat16).astype(jnp.float32)
    low = (rest - mid).astype(jnp.bfloat16).astype(jnp.float32)
    return high, mid, low


def harmonics(dir_x, dir_y, dir_z):
    sq_x = dir_x * dir_x
    sq_y = dir_y * dir_y
    sq_z = dir_z * dir_z
    return [
        jnp.full_like(dir_x, harm_zero),
        -harm_one * dir_y,
        harm_one * dir_z,
        -harm_one * dir_x,
        harm_two[0] * dir_x * dir_y,
        harm_two[1] * dir_y * dir_z,
        harm_two[2] * (2.0 * sq_z - sq_x - sq_y),
        harm_two[3] * dir_x * dir_z,
        harm_two[4] * (sq_x - sq_y),
        harm_three[0] * dir_y * (3.0 * sq_x - sq_y),
        harm_three[1] * dir_x * dir_y * dir_z,
        harm_three[2] * dir_y * (4.0 * sq_z - sq_x - sq_y),
        harm_three[3] * dir_z * (2.0 * sq_z - 3.0 * sq_x - 3.0 * sq_y),
        harm_three[4] * dir_x * (4.0 * sq_z - sq_x - sq_y),
        harm_three[5] * dir_z * (sq_x - sq_y),
        harm_three[6] * dir_x * (sq_x - 3.0 * sq_y),
    ]


def project(entries, cosine, sine_yaw):
    pos_x, pos_y, pos_z = entries[0], entries[1], entries[2]
    cam_x = cosine * pos_x - sine_yaw * pos_z
    cam_z = sine_yaw * pos_x + cosine * pos_z + distance
    inverse_z = 1.0 / cam_z
    center_u = focal_len * cam_x * inverse_z + 960.0
    center_v = focal_len * pos_y * inverse_z + 540.0
    stretch = [jnp.exp(entries[3 + axis]) for axis in range(3)]
    norm = entries[6] * entries[6] + entries[7] * entries[7]
    norm = norm + entries[8] * entries[8] + entries[9] * entries[9]
    inverse_norm = 1.0 / jnp.sqrt(norm)
    quat_w, quat_x, quat_y, quat_z = (entries[6 + part] * inverse_norm for part in range(4))
    rotation = [
        [
            1.0 - 2.0 * (quat_y * quat_y + quat_z * quat_z),
            2.0 * (quat_x * quat_y - quat_w * quat_z),
            2.0 * (quat_x * quat_z + quat_w * quat_y),
        ],
        [
            2.0 * (quat_x * quat_y + quat_w * quat_z),
            1.0 - 2.0 * (quat_x * quat_x + quat_z * quat_z),
            2.0 * (quat_y * quat_z - quat_w * quat_x),
        ],
        [
            2.0 * (quat_x * quat_z - quat_w * quat_y),
            2.0 * (quat_y * quat_z + quat_w * quat_x),
            1.0 - 2.0 * (quat_x * quat_x + quat_y * quat_y),
        ],
    ]
    focal_z = focal_len * inverse_z
    slope_x = focal_len * cam_x * inverse_z * inverse_z
    slope_y = focal_len * pos_y * inverse_z * inverse_z
    proj_u = [focal_z * cosine - slope_x * sine_yaw, None, -focal_z * sine_yaw - slope_x * cosine]
    proj_v = [-slope_y * sine_yaw, focal_z, -slope_y * cosine]
    left = [
        (proj_u[0] * rotation[0][axis] + proj_u[2] * rotation[2][axis]) * stretch[axis]
        for axis in range(3)
    ]
    right = [
        (
            proj_v[0] * rotation[0][axis]
            + proj_v[1] * rotation[1][axis]
            + proj_v[2] * rotation[2][axis]
        )
        * stretch[axis]
        for axis in range(3)
    ]
    cov_a = left[0] * left[0] + left[1] * left[1] + left[2] * left[2] + 0.3
    cov_b = left[0] * right[0] + left[1] * right[1] + left[2] * right[2]
    cov_c = right[0] * right[0] + right[1] * right[1] + right[2] * right[2] + 0.3
    determinant = cov_a * cov_c - cov_b * cov_b
    inverse_det = 1.0 / determinant
    conic_a = cov_c * inverse_det
    conic_b = -cov_b * inverse_det
    conic_c = cov_a * inverse_det
    logit = entries[10]
    tiny = logit < -80.0
    safe = jnp.where(tiny, 0.0, logit)
    log_opacity = jnp.where(tiny, logit, -jnp.log(1.0 + jnp.exp(-safe)))
    dir_x = pos_x + distance * sine_yaw
    dir_z = pos_z + distance * cosine
    inverse_len = 1.0 / jnp.sqrt(dir_x * dir_x + pos_y * pos_y + dir_z * dir_z)
    basis_set = harmonics(dir_x * inverse_len, pos_y * inverse_len, dir_z * inverse_len)
    colours = []
    for channel in range(3):
        total = basis_set[0] * entries[11 + channel]
        for term in range(1, 16):
            total = total + basis_set[term] * entries[11 + 3 * term + channel]
        total = total + 0.5
        colours.append(jnp.where(total > 0.0, total, 0.0))
    return [center_u, center_v, conic_a, conic_b, conic_c, log_opacity] + colours


def gather_columns(index, table_eight, table_one, chunks):
    low = index & (LANES - 1)
    high = lax.shift_right_logical(index, 7)
    eight = jnp.zeros((8, LANES), jnp.float32)
    one = jnp.zeros((8, LANES), jnp.float32)
    for chunk in range(chunks):
        eight = jnp.where(high == chunk, lane_take(table_eight(chunk), low), eight)
    inside = high - lax.broadcasted_iota(jnp.int32, (8, LANES), 0)
    for block in range((chunks + 7) // 8):
        one = jnp.where(inside == block * 8, lane_take(table_one(block), low), one)
    return eight, jnp.sum(one, axis=0, keepdims=True)


def lane_take(values, index):
    return jnp.take_along_axis(values, index, axis=1, mode="promise_in_bounds")


def scatter_columns(values, index, rows, total_ref):
    count = index.shape[1]
    low = index & (LANES - 1)
    high = lax.shift_right_logical(index, 7)
    low_hot = (lax.broadcasted_iota(jnp.int32, (LANES, count), 0) == low).astype(jnp.float32)
    low_hot = low_hot.astype(jnp.bfloat16)
    high_hot = lax.broadcasted_iota(jnp.int32, (rows, count), 0) == high
    pieces = [split_two(value) for value in values]
    left = [
        jnp.where(high_hot, piece[part].astype(jnp.float32), 0.0)
        for part in range(2)
        for piece in pieces
    ]
    sums = mxu(jnp.concatenate(left, axis=0).astype(jnp.bfloat16), low_hot, NT)
    total_ref[...] += sums[: QUANT * rows] + sums[QUANT * rows :]


def load_entries(params_ref, scr, rows):
    chunks = params_ref.shape[1] // LANES
    for chunk in range(chunks):
        scr[pl.ds(chunk, NPAR, stride=rows), :] = params_ref[:, chunk * LANES : (chunk + 1) * LANES]
    scr[pl.ds(chunks, NPAR, stride=rows), :] = jnp.broadcast_to(params_ref[:, 0:1], (NPAR, LANES))
    return [scr[pl.ds(row * rows, rows), :] for row in range(NPAR)]


def owner_kernel(cap, rows, params_ref, column_ref, trig_ref, eight_ref, one_ref, yaw_ref, scr, table):
    slots = column_ref.shape[1]
    chunks = params_ref.shape[1] // LANES
    for row in range(NPAR):
        scr[pl.ds(row * rows, rows), :] = jnp.ones((rows, LANES), jnp.float32)
    column = column_ref[...]
    low_hot = lax.broadcasted_iota(jnp.int32, (LANES, slots), 0) == (column & (LANES - 1))
    high_hot = lax.broadcasted_iota(jnp.int32, (rows, slots), 0) == lax.shift_right_logical(column, 7)
    asker = (lax.broadcasted_iota(jnp.int32, (1, slots), 1) // cap).astype(jnp.float32)
    who = mxu(
        jnp.where(high_hot, asker, 0.0).astype(jnp.bfloat16),
        low_hot.astype(jnp.float32).astype(jnp.bfloat16),
        NT,
    ).astype(jnp.int32)
    row_ids = lax.broadcasted_iota(jnp.int32, (rows, LANES), 0)
    lane_ids = lax.broadcasted_iota(jnp.int32, (rows, LANES), 1)
    who = jnp.where(row_ids == chunks, lane_ids, who) & (LANES - 1)
    for part in range(2):
        known = jnp.broadcast_to(trig_ref[part : part + 1, :], (8, LANES))
        for block in range(rows // 8):
            yaw_ref[part, block * 8 : block * 8 + 8, :] = lane_take(
                known, who[block * 8 : block * 8 + 8]
            )
    entries = load_entries(params_ref, scr, rows)
    for quantity, value in enumerate(project(entries, yaw_ref[0], yaw_ref[1])):
        table[pl.ds(quantity * rows, rows), :] = value

    def table_eight(chunk):
        return table[pl.ds(chunk, 8, stride=rows), :]

    def table_one(block):
        return table[pl.ds(8 * rows + block * 8, 8), :]

    @pl.loop(0, slots // LANES)
    def _(part):
        place = pl.ds(pl.multiple_of(part * LANES, LANES), LANES)
        index = jnp.broadcast_to(column_ref[:, place], (8, LANES))
        eight, one = gather_columns(index, table_eight, table_one, chunks + 1)
        eight_ref[:, place] = eight
        one_ref[:, place] = one


def tile_kernel(
    eight_ref,
    one_ref,
    slots_ref,
    rank_ref,
    anchor_ref,
    target_ref,
    out_ref,
    grad_eight_ref,
    grad_one_ref,
    total,
    one_table,
    *banks,
):
    tiles, length = slots_ref.shape
    slots = eight_ref.shape[1]
    chunks = slots // LANES
    rows = chunks
    total[...] = jnp.zeros_like(total)
    for chunk in range(chunks):
        one_table[chunk : chunk + 1, :] = one_ref[:, chunk * LANES : (chunk + 1) * LANES]

    def basis(shape, pixel_axis):
        pixel = lax.broadcasted_iota(jnp.int32, shape, pixel_axis) & (PIX - 1)
        term = lax.broadcasted_iota(jnp.int32, shape, 1 - pixel_axis)
        px = (pixel & 15).astype(jnp.float32) - 7.5
        py = lax.shift_right_logical(pixel, 4).astype(jnp.float32) - 7.5
        kind = jnp.where(term < 24, term & 7, 7)
        value = jnp.where(kind == 0, 1.0, 0.0)
        value = jnp.where(kind == 1, px, value)
        value = jnp.where(kind == 2, py, value)
        value = jnp.where(kind == 3, px * px, value)
        value = jnp.where(kind == 4, px * py, value)
        value = jnp.where(kind == 5, py * py, value)
        return value.astype(jnp.bfloat16)

    basis_pixels = basis((PIX, 32), 0)
    basis_terms = basis((8, 2 * PIX), 1)
    from_ids = lax.broadcasted_iota(jnp.int32, (length, length), 0)
    to_ids = lax.broadcasted_iota(jnp.int32, (length, length), 1)
    before = (from_ids < to_ids).astype(jnp.float32).astype(jnp.bfloat16)
    after = (from_ids > to_ids).astype(jnp.float32).astype(jnp.bfloat16)

    def table_eight(chunk):
        return eight_ref[:, chunk * LANES : (chunk + 1) * LANES]

    def table_one(block):
        return one_table[block * 8 : block * 8 + 8, :]

    def work(tile, weight_ref, ratio_ref, pair, weight_pair):
        named = jnp.broadcast_to(slots_ref[pl.ds(tile, 1), :], (8, length))
        rank = jnp.broadcast_to(rank_ref[pl.ds(tile, 1), :], (8, length))
        halves = length // LANES
        ordered, eights, ones = [], [], []
        for half in range(halves):
            place = rank[:, half * LANES : (half + 1) * LANES]
            low = place & (LANES - 1)
            index = lane_take(named[:, 0:LANES], low)
            for other in range(1, halves):
                chosen = lane_take(named[:, other * LANES : (other + 1) * LANES], low)
                index = jnp.where(lax.shift_right_logical(place, 7) == other, chosen, index)
            eight, one = gather_columns(index, table_eight, table_one, chunks)
            ordered.append(index[0:1])
            eights.append(eight)
            ones.append(one)
        ordered = jnp.concatenate(ordered, axis=1)
        eight = jnp.concatenate(eights, axis=1)
        one = jnp.concatenate(ones, axis=1)
        off_u = eight[0:1] - anchor_ref[0, tile]
        off_v = eight[1:2] - anchor_ref[1, tile]
        con_a, con_b, con_c = eight[2:3], eight[3:4], eight[4:5]
        lin_x = con_a * off_u + con_b * off_v
        lin_y = con_b * off_u + con_c * off_v
        flat = eight[5:6] - 0.5 * (con_a * off_u * off_u + 2.0 * con_b * off_u * off_v + con_c * off_v * off_v)
        zero_row = jnp.zeros((1, length), jnp.float32)
        coefs = jnp.concatenate(
            [flat, lin_x, lin_y, -0.5 * con_a, -con_b, -0.5 * con_c, zero_row, zero_row], axis=0
        )
        zero_eight = jnp.zeros((8, length), jnp.float32)
        coefs = jnp.concatenate(list(split_three(coefs)) + [zero_eight], axis=0).astype(jnp.bfloat16)
        yield
        alpha = jnp.exp(mxu(basis_pixels, coefs))
        weight_ref[...] = alpha
        log_keep = jnp.log(1.0 - alpha)
        ratio_ref[...] = alpha * jnp.exp(-log_keep)
        pair[:PIX], pair[PIX:] = split_two(log_keep)
        yield
        logs = mxu(pair[...], before)
        weight = weight_ref[...] * jnp.exp(logs[:PIX] + logs[PIX:])
        weight_ref[...] = weight
        weight_pair[:PIX], weight_pair[PIX:] = split_two(weight)
        yield
        colour = jnp.concatenate([eight[6:8], one] + [zero_row] * 5, axis=0)
        col_h, col_m, col_l = split_three(colour)
        col_stack = jnp.concatenate([col_h, col_m, col_l, zero_eight], axis=0).astype(jnp.bfloat16)
        image = mxu(col_stack, weight_pair[...], NT)
        image = image[:, :PIX] + image[:, PIX:]
        image = image[0:8] + image[8:16] + image[16:24]
        wanted = []
        for channel in range(3):
            out_ref[channel, pl.ds(tile, 1), :] = image[channel : channel + 1]
            wanted.append(target_ref[channel, pl.ds(tile, 1), :])
        zero_pix = jnp.zeros((1, PIX), jnp.float32)
        wanted = jnp.concatenate(wanted + [zero_pix] * 5, axis=0)
        gradient = (image - wanted) * (1.0 / PIX)
        gr_h, gr_m, gr_l = split_three(gradient)
        zero_more = jnp.zeros((80, PIX), jnp.float32)
        gr_stack = jnp.concatenate([gr_h, gr_h, gr_h, gr_m, gr_m, gr_l, zero_more], axis=0)
        gr_turned = gr_stack.T.astype(jnp.bfloat16)
        zero_more = jnp.zeros((80, length), jnp.float32)
        col_all = jnp.concatenate([col_h, col_m, col_l, col_h, col_m, col_h, zero_more], axis=0)
        col_all = col_all.astype(jnp.bfloat16)
        gr_stack = jnp.concatenate([gr_h, gr_m, gr_l, jnp.zeros((8, PIX), jnp.float32)], axis=0)
        gr_stack = jnp.concatenate([gr_stack, gr_stack], axis=1).astype(jnp.bfloat16)
        yield
        pull = mxu(gr_turned, col_all) * weight_ref[...]
        weight_ref[...] = pull
        pair[:PIX], pair[PIX:] = split_two(pull)
        d_colour = mxu(gr_stack, weight_pair[...])
        d_colour = d_colour[0:8] + d_colour[8:16] + d_colour[16:24]
        yield
        behind = mxu(pair[...], after)
        pull = weight_ref[...] - (behind[:PIX] + behind[PIX:]) * ratio_ref[...]
        weight_pair[:PIX], weight_pair[PIX:] = split_two(pull)
        yield
        moments = mxu(basis_terms, weight_pair[...])
        m_0, m_x, m_y = moments[0:1], moments[1:2], moments[2:3]
        m_xx, m_xy, m_yy = moments[3:4], moments[4:5], moments[5:6]
        shift_x = m_x - off_u * m_0
        shift_y = m_y - off_v * m_0
        values = [
            con_a * shift_x + con_b * shift_y,
            con_b * shift_x + con_c * shift_y,
            -0.5 * (m_xx - off_u * (m_x + shift_x)),
            -(m_xy - off_u * m_y - off_v * shift_x),
            -0.5 * (m_yy - off_v * (m_y + shift_y)),
            m_0,
            d_colour[0:1],
            d_colour[1:2],
            d_colour[2:3],
        ]
        scatter_columns(values, ordered, rows, total)
        yield

    lanes = len(banks) // 4

    @pl.loop(0, tiles // lanes)
    def _(turn):
        running = [
            work(turn * lanes + lane, *banks[4 * lane : 4 * lane + 4]) for lane in range(lanes)
        ]
        for _ in range(7):
            for one in running:
                next(one)

    for chunk in range(chunks):
        grad_eight_ref[:, chunk * LANES : (chunk + 1) * LANES] = total[pl.ds(chunk, 8, stride=rows), :]
        grad_one_ref[:, chunk * LANES : (chunk + 1) * LANES] = total[pl.ds(8 * rows + chunk, 1), :]


def update_kernel(
    rows,
    params_ref,
    first_ref,
    second_ref,
    column_ref,
    yaw_ref,
    eight_ref,
    one_ref,
    new_params_ref,
    new_first_ref,
    new_second_ref,
    scr,
    total,
):
    slots = column_ref.shape[1]
    chunks = params_ref.shape[1] // LANES
    for row in range(NPAR):
        scr[pl.ds(row * rows, rows), :] = jnp.ones((rows, LANES), jnp.float32)
    total[...] = jnp.zeros_like(total)
    width = 256

    @pl.loop(0, slots // width)
    def _(part):
        place = pl.ds(pl.multiple_of(part * width, width), width)
        values = [eight_ref[pl.ds(row, 1), place] for row in range(8)] + [one_ref[:, place]]
        scatter_columns(values, column_ref[:, place], rows, total)

    entries = load_entries(params_ref, scr, rows)
    pulls = [total[pl.ds(quantity * rows, rows), :] for quantity in range(QUANT)]
    size = jnp.abs(pulls[0])
    for pull in pulls[1:]:
        size = jnp.maximum(size, jnp.abs(pull))
    touched = size > 0.0
    _, pullback = jax.vjp(lambda values: project(values, yaw_ref[0], yaw_ref[1]), entries)
    (gradients,) = pullback(pulls)
    for row in range(NPAR):
        scr[pl.ds(row * rows, rows), :] = jnp.where(touched, gradients[row], 0.0)
    extra = jnp.sum(scr[pl.ds(chunks, NPAR, stride=rows), :], axis=1, keepdims=True)
    lane = lax.broadcasted_iota(jnp.int32, (NPAR, LANES), 1)
    row_index = lax.broadcasted_iota(jnp.int32, (NPAR, LANES), 0)
    rates = jnp.where(row_index < 14, 0.0025, 0.000125)
    rates = jnp.where(row_index < 11, 0.05, rates)
    rates = jnp.where(row_index < 10, 0.001, rates)
    rates = jnp.where(row_index < 6, 0.005, rates)
    rates = jnp.where(row_index < 3, 0.00016, rates)
    fix_one = 1.0 - beta_one**ADAM_STEP
    fix_two = 1.0 - beta_two**ADAM_STEP
    for chunk in range(chunks):
        place = slice(chunk * LANES, (chunk + 1) * LANES)
        gradient = scr[pl.ds(chunk, NPAR, stride=rows), :]
        if chunk == 0:
            gradient = gradient + jnp.where(lane == 0, extra, 0.0)
        moment = beta_one * first_ref[:, place] + (1.0 - beta_one) * gradient
        variance = beta_two * second_ref[:, place] + (1.0 - beta_two) * gradient * gradient
        change = rates * (moment / fix_one) / (jnp.sqrt(variance / fix_two) + adam_eps)
        new_params_ref[:, place] = params_ref[:, place] - change
        new_first_ref[:, place] = moment
        new_second_ref[:, place] = variance


def exchange_kernel(owners, render, *refs):
    count = (len(refs) - 2) // 2
    sources, landings, (send_sem, recv_sem) = refs[:count], refs[count : 2 * count], refs[2 * count :]
    me = lax.axis_index("owner") * render + lax.axis_index("render")

    def place(ref, peer):
        width = ref.shape[1] // owners
        return ref.at[:, pl.ds(pl.multiple_of(peer * width, LANES), width)]

    def where(step):
        peer = lax.rem(me + step, owners)
        return peer, {"owner": lax.div(peer, render), "render": lax.rem(peer, render)}

    barrier = pltpu.get_barrier_semaphore()
    for step in range(1, owners):
        pl.semaphore_signal(
            barrier, inc=1, device_id=where(step)[1], device_id_type=pl.DeviceIdType.MESH
        )
    pl.semaphore_wait(barrier, owners - 1)
    copies = []
    for step in range(1, owners):
        peer, device = where(step)
        for item in range(count):
            copy = pltpu.make_async_remote_copy(
                src_ref=place(sources[item], peer),
                dst_ref=place(landings[item], me),
                send_sem=send_sem.at[step, item],
                recv_sem=recv_sem.at[step, item],
                device_id=device,
                device_id_type=pl.DeviceIdType.MESH,
            )
            copy.start()
            copies.append(copy)
    for item in range(count):
        width = sources[item].shape[1] // owners
        own = pl.ds(pl.multiple_of(me * width, LANES), width)
        landings[item][:, own] = sources[item][:, own]
    for copy in copies:
        copy.wait()


def exchange(arrays, owners, render, number):
    if arrays[0].shape[1] // owners % LANES == 0:
        vmem = pl.BlockSpec(memory_space=pltpu.VMEM)
        return pl.pallas_call(
            functools.partial(exchange_kernel, owners, render),
            out_shape=[jax.ShapeDtypeStruct(each.shape, each.dtype) for each in arrays],
            in_specs=[vmem] * len(arrays),
            out_specs=[vmem] * len(arrays),
            scratch_shapes=[pltpu.SemaphoreType.DMA((owners, len(arrays)))] * 2,
            compiler_params=pltpu.CompilerParams(collective_id=number, has_side_effects=True),
            name=f"exchange_{number}",
        )(*arrays)
    counts = [each.shape[0] for each in arrays]
    values = jnp.concatenate(arrays, axis=0)
    sent = values.reshape(values.shape[0], owners, -1)
    got = lax.all_to_all(sent, ("owner", "render"), split_axis=1, concat_axis=1, tiled=True)
    got = got.reshape(values.shape)
    return [got[sum(counts[:item]) : sum(counts[: item + 1])] for item in range(len(arrays))]


def body(
    params, first_moment, second_moment, target, view_yaw, tile_ids, visible, tile_slots, depth_rank
):
    render = lax.axis_size("render")
    owners = lax.axis_size("owner") * render
    cap = visible.shape[2]
    slots = owners * cap
    held = params.shape[1]
    tiles, length = tile_slots.shape
    chunks = held // LANES
    rows = (chunks + 1 + 7) // 8 * 8
    f32 = jnp.float32
    view = tile_ids[0] // tiles_view
    spare = LANES if cap % LANES == 0 else 1
    requests = jnp.concatenate([visible[0], jnp.full((owners, spare), view, jnp.int32)], axis=1)
    (wanted,) = exchange([requests.reshape(1, -1)], owners, render, 0)
    wanted = wanted.reshape(owners, cap + spare)
    index = wanted[:, :cap]
    asker = jnp.arange(owners, dtype=jnp.int32)[:, None]
    column = jnp.where(index == 0, held + asker, index).reshape(1, slots)
    view_ids = jnp.arange(view_yaw.shape[0], dtype=jnp.int32)
    yaw = jnp.sum(jnp.where(wanted[:, cap][:, None] == view_ids[None, :], view_yaw[None, :], 0.0), axis=1)
    trig = jnp.stack([jnp.cos(yaw), jnp.sin(yaw)])
    trig = jnp.pad(trig, ((0, 6), (0, LANES - owners)))
    eight, one, yaws = pl.pallas_call(
        functools.partial(owner_kernel, cap, rows),
        out_shape=[
            jax.ShapeDtypeStruct((8, slots), f32),
            jax.ShapeDtypeStruct((1, slots), f32),
            jax.ShapeDtypeStruct((2, rows, LANES), f32),
        ],
        scratch_shapes=[pltpu.VMEM((NPAR * rows, LANES), f32), pltpu.VMEM((QUANT * rows, LANES), f32)],
        compiler_params=VMEM,
        name="owner_project",
    )(params, column, trig)
    eight, one = exchange([eight, one], owners, render, 1)
    within = tile_ids % tiles_view
    anchors = jnp.stack([within % tiles_across, within // tiles_across]).astype(f32) * 16.0 + 8.0
    vmem = pl.BlockSpec(memory_space=pltpu.VMEM)
    rendered, grad_eight, grad_one = pl.pallas_call(
        tile_kernel,
        out_shape=[
            jax.ShapeDtypeStruct(target.shape, f32),
            jax.ShapeDtypeStruct((8, slots), f32),
            jax.ShapeDtypeStruct((1, slots), f32),
        ],
        in_specs=[vmem, vmem, vmem, vmem, pl.BlockSpec(memory_space=pltpu.SMEM), vmem],
        scratch_shapes=[
            pltpu.VMEM((QUANT * slots // LANES, LANES), f32),
            pltpu.VMEM((slots // LANES, LANES), f32),
        ]
        + [
            pltpu.VMEM((PIX, length), f32),
            pltpu.VMEM((PIX, length), f32),
            pltpu.VMEM((2 * PIX, length), jnp.bfloat16),
            pltpu.VMEM((2 * PIX, length), jnp.bfloat16),
        ]
        * (2 if tiles % 2 == 0 else 1),
        compiler_params=VMEM,
        name="tile_step",
    )(eight, one, tile_slots, depth_rank, anchors, target)
    grad_eight, grad_one = exchange([grad_eight, grad_one], owners, render, 2)
    new_params, new_first, new_second = pl.pallas_call(
        functools.partial(update_kernel, rows),
        out_shape=[jax.ShapeDtypeStruct(params.shape, f32)] * 3,
        scratch_shapes=[pltpu.VMEM((NPAR * rows, LANES), f32), pltpu.VMEM((QUANT * rows, LANES), f32)],
        compiler_params=VMEM,
        name="adam_step",
    )(params, first_moment, second_moment, column, yaws, grad_eight, grad_one)
    return (new_params, new_first, new_second, rendered)


def solution(mesh):
    in_specs = (
        P(None, ("groups", "owner", "render")),
        P(None, ("groups", "owner", "render")),
        P(None, ("groups", "owner", "render")),
        P(None, ("groups", "owner", "render"), None),
        P("groups"),
        P(("groups", "owner", "render")),
        P(("groups", "owner", "render"), None, None),
        P(("groups", "owner", "render"), None),
        P(("groups", "owner", "render"), None),
    )
    out_specs = (
        P(None, ("groups", "owner", "render")),
        P(None, ("groups", "owner", "render")),
        P(None, ("groups", "owner", "render")),
        P(None, ("groups", "owner", "render"), None),
    )
    return jax.shard_map(body, mesh=mesh, in_specs=in_specs, out_specs=out_specs, check_vma=False)
```

```python
import functools

import jax
import jax.numpy as jnp
from jax import lax
from jax.experimental import pallas as pl
from jax.experimental.pallas import tpu as pltpu
from jax.sharding import PartitionSpec as P

NPAR = 59
PIX = 256
ADAM_STEP = 10
LANES = 128
QUANT = 9
SPLITS = 3

tiles_view = 8160
tiles_across = 120
focal_len = 1000.0
distance = 4.0
beta_one = 0.9
beta_two = 0.999
adam_eps = 1e-15
harm_zero = 0.28209479177387814
harm_one = 0.4886025119029199
harm_two = (
    1.0925484305920792,
    -1.0925484305920792,
    0.31539156525252005,
    -1.0925484305920792,
    0.5462742152960396,
)
harm_three = (
    -0.5900435899266435,
    2.890611442640554,
    -0.4570457994644658,
    0.3731763325901154,
    -0.4570457994644658,
    1.445305721320277,
    -0.5900435899266435,
)
VMEM = pltpu.CompilerParams(vmem_limit_bytes=56 * 1024 * 1024)
NN = (((1,), (0,)), ((), ()))
NT = (((1,), (1,)), ((), ()))


def mxu(left, right, dims=NN):
    return lax.dot_general(left, right, dims, preferred_element_type=jnp.float32)


def split_two(value):
    high = value.astype(jnp.bfloat16)
    low = (value - high.astype(jnp.float32)).astype(jnp.bfloat16)
    return high, low


def split_three(value):
    high = value.astype(jnp.bfloat16).astype(jnp.float32)
    rest = value - high
    mid = rest.astype(jnp.bfloat16).astype(jnp.float32)
    low = (rest - mid).astype(jnp.bfloat16).astype(jnp.float32)
    return high, mid, low


def harmonics(dir_x, dir_y, dir_z):
    sq_x = dir_x * dir_x
    sq_y = dir_y * dir_y
    sq_z = dir_z * dir_z
    return [
        jnp.full_like(dir_x, harm_zero),
        -harm_one * dir_y,
        harm_one * dir_z,
        -harm_one * dir_x,
        harm_two[0] * dir_x * dir_y,
        harm_two[1] * dir_y * dir_z,
        harm_two[2] * (2.0 * sq_z - sq_x - sq_y),
        harm_two[3] * dir_x * dir_z,
        harm_two[4] * (sq_x - sq_y),
        harm_three[0] * dir_y * (3.0 * sq_x - sq_y),
        harm_three[1] * dir_x * dir_y * dir_z,
        harm_three[2] * dir_y * (4.0 * sq_z - sq_x - sq_y),
        harm_three[3] * dir_z * (2.0 * sq_z - 3.0 * sq_x - 3.0 * sq_y),
        harm_three[4] * dir_x * (4.0 * sq_z - sq_x - sq_y),
        harm_three[5] * dir_z * (sq_x - sq_y),
        harm_three[6] * dir_x * (sq_x - 3.0 * sq_y),
    ]


def project(entries, cosine, sine_yaw):
    pos_x, pos_y, pos_z = entries[0], entries[1], entries[2]
    cam_x = cosine * pos_x - sine_yaw * pos_z
    cam_z = sine_yaw * pos_x + cosine * pos_z + distance
    inverse_z = 1.0 / cam_z
    center_u = focal_len * cam_x * inverse_z + 960.0
    center_v = focal_len * pos_y * inverse_z + 540.0
    stretch = [jnp.exp(entries[3 + axis]) for axis in range(3)]
    norm = entries[6] * entries[6] + entries[7] * entries[7]
    norm = norm + entries[8] * entries[8] + entries[9] * entries[9]
    inverse_norm = 1.0 / jnp.sqrt(norm)
    quat_w, quat_x, quat_y, quat_z = (entries[6 + part] * inverse_norm for part in range(4))
    rotation = [
        [
            1.0 - 2.0 * (quat_y * quat_y + quat_z * quat_z),
            2.0 * (quat_x * quat_y - quat_w * quat_z),
            2.0 * (quat_x * quat_z + quat_w * quat_y),
        ],
        [
            2.0 * (quat_x * quat_y + quat_w * quat_z),
            1.0 - 2.0 * (quat_x * quat_x + quat_z * quat_z),
            2.0 * (quat_y * quat_z - quat_w * quat_x),
        ],
        [
            2.0 * (quat_x * quat_z - quat_w * quat_y),
            2.0 * (quat_y * quat_z + quat_w * quat_x),
            1.0 - 2.0 * (quat_x * quat_x + quat_y * quat_y),
        ],
    ]
    focal_z = focal_len * inverse_z
    slope_x = focal_len * cam_x * inverse_z * inverse_z
    slope_y = focal_len * pos_y * inverse_z * inverse_z
    proj_u = [focal_z * cosine - slope_x * sine_yaw, None, -focal_z * sine_yaw - slope_x * cosine]
    proj_v = [-slope_y * sine_yaw, focal_z, -slope_y * cosine]
    left = [
        (proj_u[0] * rotation[0][axis] + proj_u[2] * rotation[2][axis]) * stretch[axis]
        for axis in range(3)
    ]
    right = [
        (
            proj_v[0] * rotation[0][axis]
            + proj_v[1] * rotation[1][axis]
            + proj_v[2] * rotation[2][axis]
        )
        * stretch[axis]
        for axis in range(3)
    ]
    cov_a = left[0] * left[0] + left[1] * left[1] + left[2] * left[2] + 0.3
    cov_b = left[0] * right[0] + left[1] * right[1] + left[2] * right[2]
    cov_c = right[0] * right[0] + right[1] * right[1] + right[2] * right[2] + 0.3
    determinant = cov_a * cov_c - cov_b * cov_b
    inverse_det = 1.0 / determinant
    conic_a = cov_c * inverse_det
    conic_b = -cov_b * inverse_det
    conic_c = cov_a * inverse_det
    logit = entries[10]
    tiny = logit < -80.0
    safe = jnp.where(tiny, 0.0, logit)
    log_opacity = jnp.where(tiny, logit, -jnp.log(1.0 + jnp.exp(-safe)))
    dir_x = pos_x + distance * sine_yaw
    dir_z = pos_z + distance * cosine
    inverse_len = 1.0 / jnp.sqrt(dir_x * dir_x + pos_y * pos_y + dir_z * dir_z)
    basis_set = harmonics(dir_x * inverse_len, pos_y * inverse_len, dir_z * inverse_len)
    colours = []
    for channel in range(3):
        total = basis_set[0] * entries[11 + channel]
        for term in range(1, 16):
            total = total + basis_set[term] * entries[11 + 3 * term + channel]
        total = total + 0.5
        colours.append(jnp.where(total > 0.0, total, 0.0))
    return [center_u, center_v, conic_a, conic_b, conic_c, log_opacity] + colours


def gather_columns(index, table_eight, table_one, chunks):
    low = index & (LANES - 1)
    high = lax.shift_right_logical(index, 7)
    eight = jnp.zeros((8, LANES), jnp.float32)
    one = jnp.zeros((8, LANES), jnp.float32)
    for chunk in range(chunks):
        eight = jnp.where(high == chunk, lane_take(table_eight(chunk), low), eight)
    inside = high - lax.broadcasted_iota(jnp.int32, (8, LANES), 0)
    for block in range((chunks + 7) // 8):
        one = jnp.where(inside == block * 8, lane_take(table_one(block), low), one)
    return eight, jnp.sum(one, axis=0, keepdims=True)


def lane_take(values, index):
    return jnp.take_along_axis(values, index, axis=1, mode="promise_in_bounds")


def scatter_columns(values, index, rows, total_ref):
    count = index.shape[1]
    low = index & (LANES - 1)
    high = lax.shift_right_logical(index, 7)
    low_hot = (lax.broadcasted_iota(jnp.int32, (LANES, count), 0) == low).astype(jnp.float32)
    low_hot = low_hot.astype(jnp.bfloat16)
    high_hot = lax.broadcasted_iota(jnp.int32, (rows, count), 0) == high
    pieces = [split_two(value) for value in values]
    left = [
        jnp.where(high_hot, piece[part].astype(jnp.float32), 0.0)
        for part in range(2)
        for piece in pieces
    ]
    sums = mxu(jnp.concatenate(left, axis=0).astype(jnp.bfloat16), low_hot, NT)
    total_ref[...] += sums[: QUANT * rows] + sums[QUANT * rows :]


def clear_entries(scr, rows):
    for row in range(NPAR):
        scr[pl.ds(row * rows + rows - 8, 8), :] = jnp.ones((8, LANES), jnp.float32)


def load_entries(params_ref, scr, rows):
    chunks = params_ref.shape[1] // LANES
    for chunk in range(chunks):
        scr[pl.ds(chunk, NPAR, stride=rows), :] = params_ref[:, chunk * LANES : (chunk + 1) * LANES]
    scr[pl.ds(chunks, NPAR, stride=rows), :] = jnp.broadcast_to(params_ref[:, 0:1], (NPAR, LANES))
    return [scr[pl.ds(row * rows, rows), :] for row in range(NPAR)]


class Peers:
    def __init__(self, owners, render):
        self.owners, self.render = owners, render
        self.me = lax.axis_index("owner") * render + lax.axis_index("render")

    def peer(self, step):
        return lax.rem(self.me + step, self.owners)

    def device(self, step):
        peer = self.peer(step)
        return {"owner": lax.div(peer, self.render), "render": lax.rem(peer, self.render)}

    def greet(self):
        barrier = pltpu.get_barrier_semaphore()
        for step in range(1, self.owners):
            pl.semaphore_signal(
                barrier, inc=1, device_id=self.device(step), device_id_type=pl.DeviceIdType.MESH
            )

    def met(self):
        pl.semaphore_wait(pltpu.get_barrier_semaphore(), self.owners - 1)

    def place(self, ref, peer):
        width = ref.shape[1] // self.owners
        return ref.at[:, pl.ds(pl.multiple_of(peer * width, LANES), width)]

    def copy(self, source, landing, sems, step, item):
        return pltpu.make_async_remote_copy(
            src_ref=self.place(source, self.peer(step)),
            dst_ref=self.place(landing, self.me),
            send_sem=sems[0].at[step, item],
            recv_sem=sems[1].at[step, item],
            device_id=self.device(step),
            device_id_type=pl.DeviceIdType.MESH,
        )

    def keep(self, source, landing):
        self.place(landing, self.me)[...] = self.place(source, self.me)[...]


def project_all(cap, rows, params_ref, column_ref, views, trig, yaw_ref, scr, table):
    slots = column_ref.shape[1]
    chunks = params_ref.shape[1] // LANES
    column = column_ref[...]
    low_hot = lax.broadcasted_iota(jnp.int32, (LANES, slots), 0) == (column & (LANES - 1))
    high_hot = lax.broadcasted_iota(jnp.int32, (rows, slots), 0) == lax.shift_right_logical(column, 7)
    asker = (lax.broadcasted_iota(jnp.int32, (1, slots), 1) // cap).astype(jnp.float32)
    who = mxu(
        jnp.where(high_hot, asker, 0.0).astype(jnp.bfloat16),
        low_hot.astype(jnp.float32).astype(jnp.bfloat16),
        NT,
    ).astype(jnp.int32)
    row_ids = lax.broadcasted_iota(jnp.int32, (rows, LANES), 0)
    lane_ids = lax.broadcasted_iota(jnp.int32, (rows, LANES), 1)
    who = jnp.where(row_ids == chunks, lane_ids, who) & (LANES - 1)
    known = lane_take(trig, jnp.broadcast_to(views, (8, LANES)))
    for part in range(2):
        row = jnp.broadcast_to(known[part : part + 1, :], (8, LANES))
        for block in range(rows // 8):
            yaw_ref[part, block * 8 : block * 8 + 8, :] = lane_take(
                row, who[block * 8 : block * 8 + 8]
            )
    entries = [scr[pl.ds(row * rows, rows), :] for row in range(NPAR)]
    for quantity, value in enumerate(project(entries, yaw_ref[0], yaw_ref[1])):
        table[pl.ds(quantity * rows, rows), :] = value


def look_up(rows, chunks, column_ref, place, eight_ref, one_ref, table):
    def table_eight(chunk):
        return table[pl.ds(chunk, 8, stride=rows), :]

    def table_one(block):
        return table[pl.ds(8 * rows + block * 8, 8), :]

    index = jnp.broadcast_to(column_ref[:, place], (8, LANES))
    eight_ref[:, place], one_ref[:, place] = gather_columns(
        index, table_eight, table_one, chunks + 1
    )


def owner_kernel(
    cap, rows, params_ref, column_ref, views_ref, trig_ref, eight_ref, one_ref, yaw_ref, scr, table
):
    slots = column_ref.shape[1]
    chunks = params_ref.shape[1] // LANES
    clear_entries(scr, rows)
    load_entries(params_ref, scr, rows)
    project_all(
        cap, rows, params_ref, column_ref, views_ref[...], trig_ref[...], yaw_ref, scr, table
    )

    @pl.loop(0, slots // LANES)
    def _(part):
        place = pl.ds(pl.multiple_of(part * LANES, LANES), LANES)
        look_up(rows, chunks, column_ref, place, eight_ref, one_ref, table)


def owner_exchange_kernel(
    owners,
    render,
    cap,
    rows,
    params_ref,
    request_ref,
    trig_ref,
    eight_ref,
    one_ref,
    yaw_ref,
    column_ref,
    scr,
    table,
    got,
    eight_sent,
    one_sent,
    *sems,
):
    peers = Peers(owners, render)
    peers.greet()
    held = params_ref.shape[1]
    chunks = held // LANES
    width = request_ref.shape[1] // owners
    clear_entries(scr, rows)
    peers.met()
    asked = [peers.copy(request_ref, got, sems[:2], step, 0) for step in range(1, owners)]
    for copy in asked:
        copy.start()
    peers.keep(request_ref, got)
    load_entries(params_ref, scr, rows)
    for copy in asked:
        copy.wait()
    lane = lax.broadcasted_iota(jnp.int32, (1, LANES), 1)
    views = jnp.zeros((1, LANES), jnp.int32)
    for peer in range(owners):
        index = got[:, peer * width : peer * width + cap]
        column_ref[:, peer * cap : (peer + 1) * cap] = jnp.where(index == 0, held + peer, index)
        views = jnp.where(lane == peer, got[:, peer * width + cap : (peer + 1) * width], views)
    project_all(cap, rows, params_ref, column_ref, views, trig_ref[...], yaw_ref, scr, table)

    def block(peer):
        for part in range(cap // LANES):
            place = pl.ds(pl.multiple_of(peer * cap + part * LANES, LANES), LANES)
            look_up(rows, chunks, column_ref, place, eight_sent, one_sent, table)

    def pairs(step):
        return [
            peers.copy(eight_sent, eight_ref, sems[2:], step, 0),
            peers.copy(one_sent, one_ref, sems[2:], step, 1),
        ]

    @pl.loop(1, owners)
    def _(step):
        block(peers.peer(step))
        for copy in pairs(step):
            copy.start()

    block(peers.me)
    peers.keep(eight_sent, eight_ref)
    peers.keep(one_sent, one_ref)
    for step in range(1, owners):
        for copy in pairs(step):
            copy.wait()


def tile_kernel(
    owners,
    render,
    eight_ref,
    one_ref,
    slots_ref,
    rank_ref,
    anchor_ref,
    target_ref,
    out_ref,
    grad_eight_ref,
    grad_one_ref,
    total,
    one_table,
    *banks,
):
    fused = owners > 0
    if fused:
        *banks, eight_sent, one_sent, send_sem, recv_sem = banks
        sems = (send_sem, recv_sem)
        peers = Peers(owners, render)
        peers.greet()
    else:
        eight_sent, one_sent = grad_eight_ref, grad_one_ref
    tiles, length = slots_ref.shape
    slots = eight_ref.shape[1]
    chunks = slots // LANES
    rows = chunks
    total[...] = jnp.zeros_like(total)
    for chunk in range(chunks):
        one_table[chunk : chunk + 1, :] = one_ref[:, chunk * LANES : (chunk + 1) * LANES]

    def basis(shape, pixel_axis):
        pixel = lax.broadcasted_iota(jnp.int32, shape, pixel_axis) & (PIX - 1)
        term = lax.broadcasted_iota(jnp.int32, shape, 1 - pixel_axis)
        px = (pixel & 15).astype(jnp.float32) - 7.5
        py = lax.shift_right_logical(pixel, 4).astype(jnp.float32) - 7.5
        kind = jnp.where(term < 24, term & 7, 7)
        value = jnp.where(kind == 0, 1.0, 0.0)
        value = jnp.where(kind == 1, px, value)
        value = jnp.where(kind == 2, py, value)
        value = jnp.where(kind == 3, px * px, value)
        value = jnp.where(kind == 4, px * py, value)
        value = jnp.where(kind == 5, py * py, value)
        return value.astype(jnp.bfloat16)

    basis_pixels = basis((PIX, 32), 0)
    basis_terms = basis((8, 2 * PIX), 1)
    from_ids = lax.broadcasted_iota(jnp.int32, (length, length), 0)
    to_ids = lax.broadcasted_iota(jnp.int32, (length, length), 1)
    before = (from_ids < to_ids).astype(jnp.float32).astype(jnp.bfloat16)
    after = (from_ids > to_ids).astype(jnp.float32).astype(jnp.bfloat16)

    def table_eight(chunk):
        return eight_ref[:, chunk * LANES : (chunk + 1) * LANES]

    def table_one(block):
        return one_table[block * 8 : block * 8 + 8, :]

    def work(tile, weight_ref, ratio_ref, pair, weight_pair):
        named = jnp.broadcast_to(slots_ref[pl.ds(tile, 1), :], (8, length))
        rank = jnp.broadcast_to(rank_ref[pl.ds(tile, 1), :], (8, length))
        halves = length // LANES
        ordered, eights, ones = [], [], []
        for half in range(halves):
            place = rank[:, half * LANES : (half + 1) * LANES]
            low = place & (LANES - 1)
            index = lane_take(named[:, 0:LANES], low)
            for other in range(1, halves):
                chosen = lane_take(named[:, other * LANES : (other + 1) * LANES], low)
                index = jnp.where(lax.shift_right_logical(place, 7) == other, chosen, index)
            eight, one = gather_columns(index, table_eight, table_one, chunks)
            ordered.append(index[0:1])
            eights.append(eight)
            ones.append(one)
        ordered = jnp.concatenate(ordered, axis=1)
        eight = jnp.concatenate(eights, axis=1)
        one = jnp.concatenate(ones, axis=1)
        off_u = eight[0:1] - anchor_ref[0, tile]
        off_v = eight[1:2] - anchor_ref[1, tile]
        con_a, con_b, con_c = eight[2:3], eight[3:4], eight[4:5]
        lin_x = con_a * off_u + con_b * off_v
        lin_y = con_b * off_u + con_c * off_v
        flat = eight[5:6] - 0.5 * (con_a * off_u * off_u + 2.0 * con_b * off_u * off_v + con_c * off_v * off_v)
        zero_row = jnp.zeros((1, length), jnp.float32)
        coefs = jnp.concatenate(
            [flat, lin_x, lin_y, -0.5 * con_a, -con_b, -0.5 * con_c, zero_row, zero_row], axis=0
        )
        zero_eight = jnp.zeros((8, length), jnp.float32)
        coefs = jnp.concatenate(list(split_three(coefs)) + [zero_eight], axis=0).astype(jnp.bfloat16)
        yield
        alpha = jnp.exp(mxu(basis_pixels, coefs))
        weight_ref[...] = alpha
        log_keep = jnp.log(1.0 - alpha)
        ratio_ref[...] = alpha * jnp.exp(-log_keep)
        pair[:PIX], pair[PIX:] = split_two(log_keep)
        yield
        logs = mxu(pair[...], before)
        weight = weight_ref[...] * jnp.exp(logs[:PIX] + logs[PIX:])
        weight_ref[...] = weight
        weight_pair[:PIX], weight_pair[PIX:] = split_two(weight)
        yield
        colour = jnp.concatenate([eight[6:8], one] + [zero_row] * 5, axis=0)
        col_h, col_m, col_l = split_three(colour)
        col_stack = jnp.concatenate([col_h, col_m, col_l, zero_eight], axis=0).astype(jnp.bfloat16)
        image = mxu(col_stack, weight_pair[...], NT)
        image = image[:, :PIX] + image[:, PIX:]
        image = image[0:8] + image[8:16] + image[16:24]
        wanted = []
        for channel in range(3):
            out_ref[channel, pl.ds(tile, 1), :] = image[channel : channel + 1]
            wanted.append(target_ref[channel, pl.ds(tile, 1), :])
        zero_pix = jnp.zeros((1, PIX), jnp.float32)
        wanted = jnp.concatenate(wanted + [zero_pix] * 5, axis=0)
        gradient = (image - wanted) * (1.0 / PIX)
        gr_h, gr_m, gr_l = split_three(gradient)
        zero_more = jnp.zeros((80, PIX), jnp.float32)
        gr_stack = jnp.concatenate([gr_h, gr_h, gr_h, gr_m, gr_m, gr_l, zero_more], axis=0)
        gr_turned = gr_stack.T.astype(jnp.bfloat16)
        zero_more = jnp.zeros((80, length), jnp.float32)
        col_all = jnp.concatenate([col_h, col_m, col_l, col_h, col_m, col_h, zero_more], axis=0)
        col_all = col_all.astype(jnp.bfloat16)
        gr_stack = jnp.concatenate([gr_h, gr_m, gr_l, jnp.zeros((8, PIX), jnp.float32)], axis=0)
        gr_stack = jnp.concatenate([gr_stack, gr_stack], axis=1).astype(jnp.bfloat16)
        yield
        pull = mxu(gr_turned, col_all) * weight_ref[...]
        weight_ref[...] = pull
        pair[:PIX], pair[PIX:] = split_two(pull)
        d_colour = mxu(gr_stack, weight_pair[...])
        d_colour = d_colour[0:8] + d_colour[8:16] + d_colour[16:24]
        yield
        behind = mxu(pair[...], after)
        pull = weight_ref[...] - (behind[:PIX] + behind[PIX:]) * ratio_ref[...]
        weight_pair[:PIX], weight_pair[PIX:] = split_two(pull)
        yield
        moments = mxu(basis_terms, weight_pair[...])
        m_0, m_x, m_y = moments[0:1], moments[1:2], moments[2:3]
        m_xx, m_xy, m_yy = moments[3:4], moments[4:5], moments[5:6]
        shift_x = m_x - off_u * m_0
        shift_y = m_y - off_v * m_0
        values = [
            con_a * shift_x + con_b * shift_y,
            con_b * shift_x + con_c * shift_y,
            -0.5 * (m_xx - off_u * (m_x + shift_x)),
            -(m_xy - off_u * m_y - off_v * shift_x),
            -0.5 * (m_yy - off_v * (m_y + shift_y)),
            m_0,
            d_colour[0:1],
            d_colour[1:2],
            d_colour[2:3],
        ]
        scatter_columns(values, ordered, rows, total)
        yield

    lanes = len(banks) // 4

    @pl.loop(0, tiles // lanes)
    def _(turn):
        running = [
            work(turn * lanes + lane, *banks[4 * lane : 4 * lane + 4]) for lane in range(lanes)
        ]
        for _ in range(7):
            for one in running:
                next(one)

    for chunk in range(chunks):
        eight_sent[:, chunk * LANES : (chunk + 1) * LANES] = total[pl.ds(chunk, 8, stride=rows), :]
        one_sent[:, chunk * LANES : (chunk + 1) * LANES] = total[pl.ds(8 * rows + chunk, 1), :]
    if fused:
        peers.met()
        copies = []
        for step in range(1, owners):
            copies.append(peers.copy(eight_sent, grad_eight_ref, sems, step, 0))
            copies.append(peers.copy(one_sent, grad_one_ref, sems, step, 1))
        for copy in copies:
            copy.start()
        peers.keep(eight_sent, grad_eight_ref)
        peers.keep(one_sent, grad_one_ref)
        for copy in copies:
            copy.wait()


def update_kernel(
    rows,
    params_ref,
    first_hbm,
    second_hbm,
    column_ref,
    yaw_ref,
    eight_ref,
    one_ref,
    new_params_ref,
    new_first_ref,
    new_second_ref,
    scr,
    total,
    first_ref,
    second_ref,
    load_sem,
):
    slots = column_ref.shape[1]
    chunks = params_ref.shape[1] // LANES
    clear_entries(scr, rows)
    total[...] = jnp.zeros_like(total)
    width = 256
    moments_in = [
        pltpu.make_async_copy(first_hbm, first_ref, load_sem.at[0]),
        pltpu.make_async_copy(second_hbm, second_ref, load_sem.at[1]),
    ]
    for copy in moments_in:
        copy.start()

    @pl.loop(0, slots // width)
    def _(part):
        place = pl.ds(pl.multiple_of(part * width, width), width)
        values = [eight_ref[pl.ds(row, 1), place] for row in range(8)] + [one_ref[:, place]]
        scatter_columns(values, column_ref[:, place], rows, total)

    entries = load_entries(params_ref, scr, rows)
    pulls = [total[pl.ds(quantity * rows, rows), :] for quantity in range(QUANT)]
    size = jnp.abs(pulls[0])
    for pull in pulls[1:]:
        size = jnp.maximum(size, jnp.abs(pull))
    touched = size > 0.0
    _, pullback = jax.vjp(lambda values: project(values, yaw_ref[0], yaw_ref[1]), entries)
    (gradients,) = pullback(pulls)
    for row in range(NPAR):
        scr[pl.ds(row * rows, rows), :] = jnp.where(touched, gradients[row], 0.0)
    extra = jnp.sum(scr[pl.ds(chunks, NPAR, stride=rows), :], axis=1, keepdims=True)
    lane = lax.broadcasted_iota(jnp.int32, (NPAR, LANES), 1)
    row_index = lax.broadcasted_iota(jnp.int32, (NPAR, LANES), 0)
    rates = jnp.where(row_index < 14, 0.0025, 0.000125)
    rates = jnp.where(row_index < 11, 0.05, rates)
    rates = jnp.where(row_index < 10, 0.001, rates)
    rates = jnp.where(row_index < 6, 0.005, rates)
    rates = jnp.where(row_index < 3, 0.00016, rates)
    fix_one = 1.0 - beta_one**ADAM_STEP
    fix_two = 1.0 - beta_two**ADAM_STEP
    for copy in moments_in:
        copy.wait()
    for chunk in range(chunks):
        place = slice(chunk * LANES, (chunk + 1) * LANES)
        gradient = scr[pl.ds(chunk, NPAR, stride=rows), :]
        if chunk == 0:
            gradient = gradient + jnp.where(lane == 0, extra, 0.0)
        moment = beta_one * first_ref[:, place] + (1.0 - beta_one) * gradient
        variance = beta_two * second_ref[:, place] + (1.0 - beta_two) * gradient * gradient
        change = rates * (moment / fix_one) / (jnp.sqrt(variance / fix_two) + adam_eps)
        new_params_ref[:, place] = params_ref[:, place] - change
        new_first_ref[:, place] = moment
        new_second_ref[:, place] = variance


def exchange(arrays, owners):
    counts = [each.shape[0] for each in arrays]
    values = jnp.concatenate(arrays, axis=0)
    sent = values.reshape(values.shape[0], owners, -1)
    got = lax.all_to_all(sent, ("owner", "render"), split_axis=1, concat_axis=1, tiled=True)
    got = got.reshape(values.shape)
    return [got[sum(counts[:item]) : sum(counts[: item + 1])] for item in range(len(arrays))]


def body(
    params, first_moment, second_moment, target, view_yaw, tile_ids, visible, tile_slots, depth_rank
):
    render = lax.axis_size("render")
    owners = lax.axis_size("owner") * render
    cap = visible.shape[2]
    slots = owners * cap
    held = params.shape[1]
    tiles, length = tile_slots.shape
    chunks = held // LANES
    rows = (chunks + 1 + 7) // 8 * 8
    f32 = jnp.float32
    view = tile_ids[0] // tiles_view
    vmem = pl.BlockSpec(memory_space=pltpu.VMEM)
    fused = cap % LANES == 0
    trig = jnp.stack([jnp.cos(view_yaw), jnp.sin(view_yaw)])
    trig = jnp.pad(trig, ((0, 6), (0, LANES - view_yaw.shape[0])))
    spare = LANES if fused else 1
    requests = jnp.concatenate([visible[0], jnp.full((owners, spare), view, jnp.int32)], axis=1)
    requests = requests.reshape(1, -1)
    shared = [
        jax.ShapeDtypeStruct((8, slots), f32),
        jax.ShapeDtypeStruct((1, slots), f32),
        jax.ShapeDtypeStruct((2, rows, LANES), f32),
    ]
    room = [pltpu.VMEM((NPAR * rows, LANES), f32), pltpu.VMEM((QUANT * rows, LANES), f32)]
    sends = [pltpu.VMEM((8, slots), f32), pltpu.VMEM((1, slots), f32)]
    sems = [pltpu.SemaphoreType.DMA((owners, 2))] * 2
    if fused:
        eight, one, yaws, column = pl.pallas_call(
            functools.partial(owner_exchange_kernel, owners, render, cap, rows),
            out_shape=shared + [jax.ShapeDtypeStruct((1, slots), jnp.int32)],
            in_specs=[vmem] * 3,
            out_specs=[vmem] * 4,
            scratch_shapes=room + [pltpu.VMEM(requests.shape, jnp.int32)] + sends + sems + sems,
            compiler_params=pltpu.CompilerParams(
                vmem_limit_bytes=56 * 1024 * 1024, collective_id=0, has_side_effects=True
            ),
            name="owner_project",
        )(params, requests, trig)
    else:
        (wanted,) = exchange([requests], owners)
        wanted = wanted.reshape(owners, cap + spare)
        index = wanted[:, :cap]
        asker = jnp.arange(owners, dtype=jnp.int32)[:, None]
        column = jnp.where(index == 0, held + asker, index).reshape(1, slots)
        views = jnp.pad(wanted[:, cap], (0, LANES - owners)).reshape(1, LANES)
        eight, one, yaws = pl.pallas_call(
            functools.partial(owner_kernel, cap, rows),
            out_shape=shared,
            scratch_shapes=room,
            compiler_params=VMEM,
            name="owner_project",
        )(params, column, views, trig)
        eight, one = exchange([eight, one], owners)
    within = tile_ids % tiles_view
    anchors = jnp.stack([within % tiles_across, within // tiles_across]).astype(f32) * 16.0 + 8.0
    rendered, grad_eight, grad_one = pl.pallas_call(
        functools.partial(tile_kernel, owners if fused else 0, render),
        out_shape=[
            jax.ShapeDtypeStruct(target.shape, f32),
            jax.ShapeDtypeStruct((8, slots), f32),
            jax.ShapeDtypeStruct((1, slots), f32),
        ],
        in_specs=[vmem, vmem, vmem, vmem, pl.BlockSpec(memory_space=pltpu.SMEM), vmem],
        scratch_shapes=[
            pltpu.VMEM((QUANT * slots // LANES, LANES), f32),
            pltpu.VMEM((slots // LANES, LANES), f32),
        ]
        + [
            pltpu.VMEM((PIX, length), f32),
            pltpu.VMEM((PIX, length), f32),
            pltpu.VMEM((2 * PIX, length), jnp.bfloat16),
            pltpu.VMEM((2 * PIX, length), jnp.bfloat16),
        ]
        * (2 if tiles % 2 == 0 else 1)
        + (sends + sems if fused else []),
        compiler_params=pltpu.CompilerParams(
            vmem_limit_bytes=56 * 1024 * 1024, collective_id=1, has_side_effects=True
        )
        if fused
        else VMEM,
        name="tile_step",
    )(eight, one, tile_slots, depth_rank, anchors, target)
    if not fused:
        grad_eight, grad_one = exchange([grad_eight, grad_one], owners)
    hbm = pl.BlockSpec(memory_space=pl.ANY)
    new_params, new_first, new_second = pl.pallas_call(
        functools.partial(update_kernel, rows),
        out_shape=[jax.ShapeDtypeStruct(params.shape, f32)] * 3,
        in_specs=[vmem, hbm, hbm, vmem, vmem, vmem, vmem],
        scratch_shapes=room
        + [
            pltpu.VMEM(params.shape, f32),
            pltpu.VMEM(params.shape, f32),
            pltpu.SemaphoreType.DMA((2,)),
        ],
        compiler_params=VMEM,
        name="adam_step",
    )(params, first_moment, second_moment, column, yaws, grad_eight, grad_one)
    return (new_params, new_first, new_second, rendered)


def solution(mesh):
    in_specs = (
        P(None, ("groups", "owner", "render")),
        P(None, ("groups", "owner", "render")),
        P(None, ("groups", "owner", "render")),
        P(None, ("groups", "owner", "render"), None),
        P("groups"),
        P(("groups", "owner", "render")),
        P(("groups", "owner", "render"), None, None),
        P(("groups", "owner", "render"), None),
        P(("groups", "owner", "render"), None),
    )
    out_specs = (
        P(None, ("groups", "owner", "render")),
        P(None, ("groups", "owner", "render")),
        P(None, ("groups", "owner", "render")),
        P(None, ("groups", "owner", "render"), None),
    )
    return jax.shard_map(body, mesh=mesh, in_specs=in_specs, out_specs=out_specs, check_vma=False)
```

```python
import functools

import jax
import jax.numpy as jnp
from jax import lax
from jax.experimental import pallas as pl
from jax.experimental.pallas import tpu as pltpu
from jax.sharding import PartitionSpec as P

NPAR = 59
PIX = 256
ADAM_STEP = 10
LANES = 128
QUANT = 9
SPLITS = 3

tiles_view = 8160
tiles_across = 120
focal_len = 1000.0
distance = 4.0
beta_one = 0.9
beta_two = 0.999
adam_eps = 1e-15
harm_zero = 0.28209479177387814
harm_one = 0.4886025119029199
harm_two = (
    1.0925484305920792,
    -1.0925484305920792,
    0.31539156525252005,
    -1.0925484305920792,
    0.5462742152960396,
)
harm_three = (
    -0.5900435899266435,
    2.890611442640554,
    -0.4570457994644658,
    0.3731763325901154,
    -0.4570457994644658,
    1.445305721320277,
    -0.5900435899266435,
)
VMEM = pltpu.CompilerParams(vmem_limit_bytes=56 * 1024 * 1024)
NN = (((1,), (0,)), ((), ()))
NT = (((1,), (1,)), ((), ()))


def mxu(left, right, dims=NN):
    return lax.dot_general(left, right, dims, preferred_element_type=jnp.float32)


def split_two(value):
    high = value.astype(jnp.bfloat16)
    low = (value - high.astype(jnp.float32)).astype(jnp.bfloat16)
    return high, low


def split_three(value):
    high = value.astype(jnp.bfloat16).astype(jnp.float32)
    rest = value - high
    mid = rest.astype(jnp.bfloat16).astype(jnp.float32)
    low = (rest - mid).astype(jnp.bfloat16).astype(jnp.float32)
    return high, mid, low


def harmonics(dir_x, dir_y, dir_z):
    sq_x = dir_x * dir_x
    sq_y = dir_y * dir_y
    sq_z = dir_z * dir_z
    return [
        jnp.full_like(dir_x, harm_zero),
        -harm_one * dir_y,
        harm_one * dir_z,
        -harm_one * dir_x,
        harm_two[0] * dir_x * dir_y,
        harm_two[1] * dir_y * dir_z,
        harm_two[2] * (2.0 * sq_z - sq_x - sq_y),
        harm_two[3] * dir_x * dir_z,
        harm_two[4] * (sq_x - sq_y),
        harm_three[0] * dir_y * (3.0 * sq_x - sq_y),
        harm_three[1] * dir_x * dir_y * dir_z,
        harm_three[2] * dir_y * (4.0 * sq_z - sq_x - sq_y),
        harm_three[3] * dir_z * (2.0 * sq_z - 3.0 * sq_x - 3.0 * sq_y),
        harm_three[4] * dir_x * (4.0 * sq_z - sq_x - sq_y),
        harm_three[5] * dir_z * (sq_x - sq_y),
        harm_three[6] * dir_x * (sq_x - 3.0 * sq_y),
    ]


def project(entries, cosine, sine_yaw):
    pos_x, pos_y, pos_z = entries[0], entries[1], entries[2]
    cam_x = cosine * pos_x - sine_yaw * pos_z
    cam_z = sine_yaw * pos_x + cosine * pos_z + distance
    inverse_z = 1.0 / cam_z
    center_u = focal_len * cam_x * inverse_z + 960.0
    center_v = focal_len * pos_y * inverse_z + 540.0
    stretch = [jnp.exp(entries[3 + axis]) for axis in range(3)]
    norm = entries[6] * entries[6] + entries[7] * entries[7]
    norm = norm + entries[8] * entries[8] + entries[9] * entries[9]
    inverse_norm = 1.0 / jnp.sqrt(norm)
    quat_w, quat_x, quat_y, quat_z = (entries[6 + part] * inverse_norm for part in range(4))
    rotation = [
        [
            1.0 - 2.0 * (quat_y * quat_y + quat_z * quat_z),
            2.0 * (quat_x * quat_y - quat_w * quat_z),
            2.0 * (quat_x * quat_z + quat_w * quat_y),
        ],
        [
            2.0 * (quat_x * quat_y + quat_w * quat_z),
            1.0 - 2.0 * (quat_x * quat_x + quat_z * quat_z),
            2.0 * (quat_y * quat_z - quat_w * quat_x),
        ],
        [
            2.0 * (quat_x * quat_z - quat_w * quat_y),
            2.0 * (quat_y * quat_z + quat_w * quat_x),
            1.0 - 2.0 * (quat_x * quat_x + quat_y * quat_y),
        ],
    ]
    focal_z = focal_len * inverse_z
    slope_x = focal_len * cam_x * inverse_z * inverse_z
    slope_y = focal_len * pos_y * inverse_z * inverse_z
    proj_u = [focal_z * cosine - slope_x * sine_yaw, None, -focal_z * sine_yaw - slope_x * cosine]
    proj_v = [-slope_y * sine_yaw, focal_z, -slope_y * cosine]
    left = [
        (proj_u[0] * rotation[0][axis] + proj_u[2] * rotation[2][axis]) * stretch[axis]
        for axis in range(3)
    ]
    right = [
        (
            proj_v[0] * rotation[0][axis]
            + proj_v[1] * rotation[1][axis]
            + proj_v[2] * rotation[2][axis]
        )
        * stretch[axis]
        for axis in range(3)
    ]
    cov_a = left[0] * left[0] + left[1] * left[1] + left[2] * left[2] + 0.3
    cov_b = left[0] * right[0] + left[1] * right[1] + left[2] * right[2]
    cov_c = right[0] * right[0] + right[1] * right[1] + right[2] * right[2] + 0.3
    determinant = cov_a * cov_c - cov_b * cov_b
    inverse_det = 1.0 / determinant
    conic_a = cov_c * inverse_det
    conic_b = -cov_b * inverse_det
    conic_c = cov_a * inverse_det
    logit = entries[10]
    tiny = logit < -80.0
    safe = jnp.where(tiny, 0.0, logit)
    log_opacity = jnp.where(tiny, logit, -jnp.log(1.0 + jnp.exp(-safe)))
    dir_x = pos_x + distance * sine_yaw
    dir_z = pos_z + distance * cosine
    inverse_len = 1.0 / jnp.sqrt(dir_x * dir_x + pos_y * pos_y + dir_z * dir_z)
    basis_set = harmonics(dir_x * inverse_len, pos_y * inverse_len, dir_z * inverse_len)
    colours = []
    for channel in range(3):
        total = basis_set[0] * entries[11 + channel]
        for term in range(1, 16):
            total = total + basis_set[term] * entries[11 + 3 * term + channel]
        total = total + 0.5
        colours.append(jnp.where(total > 0.0, total, 0.0))
    return [center_u, center_v, conic_a, conic_b, conic_c, log_opacity] + colours


def gather_columns(index, table_eight, table_one, chunks):
    low = index & (LANES - 1)
    high = lax.shift_right_logical(index, 7)
    eight = jnp.zeros((8, LANES), jnp.float32)
    one = jnp.zeros((8, LANES), jnp.float32)
    for chunk in range(chunks):
        eight = jnp.where(high == chunk, lane_take(table_eight(chunk), low), eight)
    inside = high - lax.broadcasted_iota(jnp.int32, (8, LANES), 0)
    for block in range((chunks + 7) // 8):
        one = jnp.where(inside == block * 8, lane_take(table_one(block), low), one)
    return eight, jnp.sum(one, axis=0, keepdims=True)


def lane_take(values, index):
    return jnp.take_along_axis(values, index, axis=1, mode="promise_in_bounds")


def scatter_columns(values, index, rows, total_ref):
    count = index.shape[1]
    low = index & (LANES - 1)
    high = lax.shift_right_logical(index, 7)
    low_hot = (lax.broadcasted_iota(jnp.int32, (LANES, count), 0) == low).astype(jnp.float32)
    low_hot = low_hot.astype(jnp.bfloat16)
    high_hot = lax.broadcasted_iota(jnp.int32, (rows, count), 0) == high
    pieces = [split_two(value) for value in values]
    left = [
        jnp.where(high_hot, piece[part].astype(jnp.float32), 0.0)
        for part in range(2)
        for piece in pieces
    ]
    sums = mxu(jnp.concatenate(left, axis=0).astype(jnp.bfloat16), low_hot, NT)
    total_ref[...] += sums[: QUANT * rows] + sums[QUANT * rows :]


def clear_entries(scr, rows):
    for row in range(NPAR):
        scr[pl.ds(row * rows + rows - 8, 8), :] = jnp.ones((8, LANES), jnp.float32)


def load_entries(params_ref, scr, rows):
    chunks = params_ref.shape[1] // LANES
    for chunk in range(chunks):
        scr[pl.ds(chunk, NPAR, stride=rows), :] = params_ref[:, chunk * LANES : (chunk + 1) * LANES]
    scr[pl.ds(chunks, NPAR, stride=rows), :] = jnp.broadcast_to(params_ref[:, 0:1], (NPAR, LANES))
    return [scr[pl.ds(row * rows, rows), :] for row in range(NPAR)]


class Peers:
    def __init__(self, owners, render):
        self.owners, self.render = owners, render
        self.me = lax.axis_index("owner") * render + lax.axis_index("render")

    def peer(self, step):
        return lax.rem(self.me + step, self.owners)

    def device(self, step):
        peer = self.peer(step)
        return {"owner": lax.div(peer, self.render), "render": lax.rem(peer, self.render)}

    def greet(self):
        barrier = pltpu.get_barrier_semaphore()
        for step in range(1, self.owners):
            pl.semaphore_signal(
                barrier, inc=1, device_id=self.device(step), device_id_type=pl.DeviceIdType.MESH
            )

    def met(self):
        pl.semaphore_wait(pltpu.get_barrier_semaphore(), self.owners - 1)

    def place(self, ref, peer):
        width = ref.shape[1] // self.owners
        return ref.at[:, pl.ds(pl.multiple_of(peer * width, LANES), width)]

    def copy(self, source, landing, sems, step, item):
        return pltpu.make_async_remote_copy(
            src_ref=self.place(source, self.peer(step)),
            dst_ref=self.place(landing, self.me),
            send_sem=sems[0].at[step, item],
            recv_sem=sems[1].at[step, item],
            device_id=self.device(step),
            device_id_type=pl.DeviceIdType.MESH,
        )

    def keep(self, source, landing):
        self.place(landing, self.me)[...] = self.place(source, self.me)[...]


def project_all(cap, rows, params_ref, column_ref, views, trig, yaw_ref, scr, table):
    slots = column_ref.shape[1]
    chunks = params_ref.shape[1] // LANES
    column = column_ref[...]
    low_hot = lax.broadcasted_iota(jnp.int32, (LANES, slots), 0) == (column & (LANES - 1))
    high_hot = lax.broadcasted_iota(jnp.int32, (rows, slots), 0) == lax.shift_right_logical(column, 7)
    asker = (lax.broadcasted_iota(jnp.int32, (1, slots), 1) // cap).astype(jnp.float32)
    who = mxu(
        jnp.where(high_hot, asker, 0.0).astype(jnp.bfloat16),
        low_hot.astype(jnp.float32).astype(jnp.bfloat16),
        NT,
    ).astype(jnp.int32)
    row_ids = lax.broadcasted_iota(jnp.int32, (rows, LANES), 0)
    lane_ids = lax.broadcasted_iota(jnp.int32, (rows, LANES), 1)
    who = jnp.where(row_ids == chunks, lane_ids, who) & (LANES - 1)
    known = lane_take(trig, jnp.broadcast_to(views, (8, LANES)))
    for part in range(2):
        row = jnp.broadcast_to(known[part : part + 1, :], (8, LANES))
        for block in range(rows // 8):
            yaw_ref[part, block * 8 : block * 8 + 8, :] = lane_take(
                row, who[block * 8 : block * 8 + 8]
            )
    entries = [scr[pl.ds(row * rows, rows), :] for row in range(NPAR)]
    for quantity, value in enumerate(project(entries, yaw_ref[0], yaw_ref[1])):
        table[pl.ds(quantity * rows, rows), :] = value


def look_up(rows, chunks, column_ref, place, eight_ref, one_ref, table):
    def table_eight(chunk):
        return table[pl.ds(chunk, 8, stride=rows), :]

    def table_one(block):
        return table[pl.ds(8 * rows + block * 8, 8), :]

    index = jnp.broadcast_to(column_ref[:, place], (8, LANES))
    eight_ref[:, place], one_ref[:, place] = gather_columns(
        index, table_eight, table_one, chunks + 1
    )


def owner_kernel(
    cap, rows, params_ref, column_ref, views_ref, trig_ref, eight_ref, one_ref, yaw_ref, scr, table
):
    slots = column_ref.shape[1]
    chunks = params_ref.shape[1] // LANES
    clear_entries(scr, rows)
    load_entries(params_ref, scr, rows)
    project_all(
        cap, rows, params_ref, column_ref, views_ref[...], trig_ref[...], yaw_ref, scr, table
    )

    @pl.loop(0, slots // LANES)
    def _(part):
        place = pl.ds(pl.multiple_of(part * LANES, LANES), LANES)
        look_up(rows, chunks, column_ref, place, eight_ref, one_ref, table)


def owner_exchange_kernel(
    owners,
    render,
    cap,
    rows,
    params_ref,
    visible_ref,
    yaw_in_ref,
    tile_ref,
    eight_ref,
    one_ref,
    yaw_ref,
    column_ref,
    scr,
    table,
    request_ref,
    got,
    eight_sent,
    one_sent,
    *sems,
):
    peers = Peers(owners, render)
    peers.greet()
    held = params_ref.shape[1]
    chunks = held // LANES
    width = request_ref.shape[1] // owners
    view = jnp.full((1, LANES), tile_ref[0] // tiles_view, jnp.int32)
    for peer in range(owners):
        request_ref[:, peer * width : peer * width + cap] = visible_ref[0, peer : peer + 1, :]
        request_ref[:, peer * width + cap : (peer + 1) * width] = view
    clear_entries(scr, rows)
    peers.met()
    asked = [peers.copy(request_ref, got, sems[:2], step, 0) for step in range(1, owners)]
    for copy in asked:
        copy.start()
    peers.keep(request_ref, got)
    load_entries(params_ref, scr, rows)
    side = lax.broadcasted_iota(jnp.int32, (8, LANES), 0)
    wide = lax.broadcasted_iota(jnp.int32, (8, LANES), 1)
    yaw = jnp.zeros((8, LANES), jnp.float32)
    for each in range(yaw_in_ref.shape[0]):
        yaw = jnp.where(wide == each, yaw_in_ref[each], yaw)
    trig = jnp.where(side == 0, jnp.cos(yaw), jnp.sin(yaw))
    for copy in asked:
        copy.wait()
    lane = lax.broadcasted_iota(jnp.int32, (1, LANES), 1)
    views = jnp.zeros((1, LANES), jnp.int32)
    for peer in range(owners):
        index = got[:, peer * width : peer * width + cap]
        column_ref[:, peer * cap : (peer + 1) * cap] = jnp.where(index == 0, held + peer, index)
        views = jnp.where(lane == peer, got[:, peer * width + cap : (peer + 1) * width], views)
    project_all(cap, rows, params_ref, column_ref, views, trig, yaw_ref, scr, table)

    def block(peer):
        for part in range(cap // LANES):
            place = pl.ds(pl.multiple_of(peer * cap + part * LANES, LANES), LANES)
            look_up(rows, chunks, column_ref, place, eight_sent, one_sent, table)

    def pairs(step):
        return [
            peers.copy(eight_sent, eight_ref, sems[2:], step, 0),
            peers.copy(one_sent, one_ref, sems[2:], step, 1),
        ]

    @pl.loop(1, owners)
    def _(step):
        block(peers.peer(step))
        for copy in pairs(step):
            copy.start()

    block(peers.me)
    peers.keep(eight_sent, eight_ref)
    peers.keep(one_sent, one_ref)
    for step in range(1, owners):
        for copy in pairs(step):
            copy.wait()


def tile_kernel(
    owners,
    render,
    eight_ref,
    one_ref,
    slots_ref,
    rank_ref,
    tile_ref,
    target_ref,
    out_ref,
    grad_eight_ref,
    grad_one_ref,
    total,
    one_table,
    *banks,
):
    fused = owners > 0
    if fused:
        *banks, eight_sent, one_sent, send_sem, recv_sem = banks
        sems = (send_sem, recv_sem)
        peers = Peers(owners, render)
        peers.greet()
    else:
        eight_sent, one_sent = grad_eight_ref, grad_one_ref
    tiles, length = slots_ref.shape
    slots = eight_ref.shape[1]
    chunks = slots // LANES
    rows = chunks
    total[...] = jnp.zeros_like(total)
    for chunk in range(chunks):
        one_table[chunk : chunk + 1, :] = one_ref[:, chunk * LANES : (chunk + 1) * LANES]

    def basis(shape, pixel_axis):
        pixel = lax.broadcasted_iota(jnp.int32, shape, pixel_axis) & (PIX - 1)
        term = lax.broadcasted_iota(jnp.int32, shape, 1 - pixel_axis)
        px = (pixel & 15).astype(jnp.float32) - 7.5
        py = lax.shift_right_logical(pixel, 4).astype(jnp.float32) - 7.5
        kind = jnp.where(term < 24, term & 7, 7)
        value = jnp.where(kind == 0, 1.0, 0.0)
        value = jnp.where(kind == 1, px, value)
        value = jnp.where(kind == 2, py, value)
        value = jnp.where(kind == 3, px * px, value)
        value = jnp.where(kind == 4, px * py, value)
        value = jnp.where(kind == 5, py * py, value)
        return value.astype(jnp.bfloat16)

    basis_pixels = basis((PIX, 32), 0)
    basis_terms = basis((8, 2 * PIX), 1)
    from_ids = lax.broadcasted_iota(jnp.int32, (length, length), 0)
    to_ids = lax.broadcasted_iota(jnp.int32, (length, length), 1)
    before = (from_ids < to_ids).astype(jnp.float32).astype(jnp.bfloat16)
    after = (from_ids > to_ids).astype(jnp.float32).astype(jnp.bfloat16)

    def table_eight(chunk):
        return eight_ref[:, chunk * LANES : (chunk + 1) * LANES]

    def table_one(block):
        return one_table[block * 8 : block * 8 + 8, :]

    def work(tile, weight_ref, ratio_ref, pair, weight_pair):
        named = jnp.broadcast_to(slots_ref[pl.ds(tile, 1), :], (8, length))
        rank = jnp.broadcast_to(rank_ref[pl.ds(tile, 1), :], (8, length))
        halves = length // LANES
        ordered, eights, ones = [], [], []
        for half in range(halves):
            place = rank[:, half * LANES : (half + 1) * LANES]
            low = place & (LANES - 1)
            index = lane_take(named[:, 0:LANES], low)
            for other in range(1, halves):
                chosen = lane_take(named[:, other * LANES : (other + 1) * LANES], low)
                index = jnp.where(lax.shift_right_logical(place, 7) == other, chosen, index)
            eight, one = gather_columns(index, table_eight, table_one, chunks)
            ordered.append(index[0:1])
            eights.append(eight)
            ones.append(one)
        ordered = jnp.concatenate(ordered, axis=1)
        eight = jnp.concatenate(eights, axis=1)
        one = jnp.concatenate(ones, axis=1)
        within = lax.rem(tile_ref[tile], tiles_view)
        corner_x = lax.rem(within, tiles_across) * 16
        corner_y = lax.div(within, tiles_across) * 16
        off_u = eight[0:1] - (corner_x.astype(jnp.float32) + 8.0)
        off_v = eight[1:2] - (corner_y.astype(jnp.float32) + 8.0)
        con_a, con_b, con_c = eight[2:3], eight[3:4], eight[4:5]
        lin_x = con_a * off_u + con_b * off_v
        lin_y = con_b * off_u + con_c * off_v
        flat = eight[5:6] - 0.5 * (con_a * off_u * off_u + 2.0 * con_b * off_u * off_v + con_c * off_v * off_v)
        zero_row = jnp.zeros((1, length), jnp.float32)
        coefs = jnp.concatenate(
            [flat, lin_x, lin_y, -0.5 * con_a, -con_b, -0.5 * con_c, zero_row, zero_row], axis=0
        )
        zero_eight = jnp.zeros((8, length), jnp.float32)
        coefs = jnp.concatenate(list(split_three(coefs)) + [zero_eight], axis=0).astype(jnp.bfloat16)
        yield
        alpha = jnp.exp(mxu(basis_pixels, coefs))
        weight_ref[...] = alpha
        log_keep = jnp.log(1.0 - alpha)
        ratio_ref[...] = alpha * jnp.exp(-log_keep)
        pair[:PIX], pair[PIX:] = split_two(log_keep)
        yield
        logs = mxu(pair[...], before)
        weight = weight_ref[...] * jnp.exp(logs[:PIX] + logs[PIX:])
        weight_ref[...] = weight
        weight_pair[:PIX], weight_pair[PIX:] = split_two(weight)
        yield
        colour = jnp.concatenate([eight[6:8], one] + [zero_row] * 5, axis=0)
        col_h, col_m, col_l = split_three(colour)
        col_stack = jnp.concatenate([col_h, col_m, col_l, zero_eight], axis=0).astype(jnp.bfloat16)
        image = mxu(col_stack, weight_pair[...], NT)
        image = image[:, :PIX] + image[:, PIX:]
        image = image[0:8] + image[8:16] + image[16:24]
        wanted = []
        for channel in range(3):
            out_ref[channel, pl.ds(tile, 1), :] = image[channel : channel + 1]
            wanted.append(target_ref[channel, pl.ds(tile, 1), :])
        zero_pix = jnp.zeros((1, PIX), jnp.float32)
        wanted = jnp.concatenate(wanted + [zero_pix] * 5, axis=0)
        gradient = (image - wanted) * (1.0 / PIX)
        gr_h, gr_m, gr_l = split_three(gradient)
        zero_more = jnp.zeros((80, PIX), jnp.float32)
        gr_stack = jnp.concatenate([gr_h, gr_h, gr_h, gr_m, gr_m, gr_l, zero_more], axis=0)
        gr_turned = gr_stack.T.astype(jnp.bfloat16)
        zero_more = jnp.zeros((80, length), jnp.float32)
        col_all = jnp.concatenate([col_h, col_m, col_l, col_h, col_m, col_h, zero_more], axis=0)
        col_all = col_all.astype(jnp.bfloat16)
        gr_stack = jnp.concatenate([gr_h, gr_m, gr_l, jnp.zeros((8, PIX), jnp.float32)], axis=0)
        gr_stack = jnp.concatenate([gr_stack, gr_stack], axis=1).astype(jnp.bfloat16)
        yield
        pull = mxu(gr_turned, col_all) * weight_ref[...]
        weight_ref[...] = pull
        pair[:PIX], pair[PIX:] = split_two(pull)
        d_colour = mxu(gr_stack, weight_pair[...])
        d_colour = d_colour[0:8] + d_colour[8:16] + d_colour[16:24]
        yield
        behind = mxu(pair[...], after)
        pull = weight_ref[...] - (behind[:PIX] + behind[PIX:]) * ratio_ref[...]
        weight_pair[:PIX], weight_pair[PIX:] = split_two(pull)
        yield
        moments = mxu(basis_terms, weight_pair[...])
        m_0, m_x, m_y = moments[0:1], moments[1:2], moments[2:3]
        m_xx, m_xy, m_yy = moments[3:4], moments[4:5], moments[5:6]
        shift_x = m_x - off_u * m_0
        shift_y = m_y - off_v * m_0
        values = [
            con_a * shift_x + con_b * shift_y,
            con_b * shift_x + con_c * shift_y,
            -0.5 * (m_xx - off_u * (m_x + shift_x)),
            -(m_xy - off_u * m_y - off_v * shift_x),
            -0.5 * (m_yy - off_v * (m_y + shift_y)),
            m_0,
            d_colour[0:1],
            d_colour[1:2],
            d_colour[2:3],
        ]
        scatter_columns(values, ordered, rows, total)
        yield

    lanes = len(banks) // 4

    @pl.loop(0, tiles // lanes)
    def _(turn):
        running = [
            work(turn * lanes + lane, *banks[4 * lane : 4 * lane + 4]) for lane in range(lanes)
        ]
        for _ in range(7):
            for one in running:
                next(one)

    for chunk in range(chunks):
        eight_sent[:, chunk * LANES : (chunk + 1) * LANES] = total[pl.ds(chunk, 8, stride=rows), :]
        one_sent[:, chunk * LANES : (chunk + 1) * LANES] = total[pl.ds(8 * rows + chunk, 1), :]
    if fused:
        peers.met()
        copies = []
        for step in range(1, owners):
            copies.append(peers.copy(eight_sent, grad_eight_ref, sems, step, 0))
            copies.append(peers.copy(one_sent, grad_one_ref, sems, step, 1))
        for copy in copies:
            copy.start()
        peers.keep(eight_sent, grad_eight_ref)
        peers.keep(one_sent, grad_one_ref)
        for copy in copies:
            copy.wait()


def update_kernel(
    rows,
    params_ref,
    first_hbm,
    second_hbm,
    column_ref,
    yaw_ref,
    eight_ref,
    one_ref,
    new_params_ref,
    new_first_ref,
    new_second_ref,
    scr,
    total,
    first_ref,
    second_ref,
    load_sem,
):
    slots = column_ref.shape[1]
    chunks = params_ref.shape[1] // LANES
    clear_entries(scr, rows)
    total[...] = jnp.zeros_like(total)
    width = 1024
    moments_in = [
        pltpu.make_async_copy(first_hbm, first_ref, load_sem.at[0]),
        pltpu.make_async_copy(second_hbm, second_ref, load_sem.at[1]),
    ]
    for copy in moments_in:
        copy.start()

    @pl.loop(0, slots // width)
    def _(part):
        place = pl.ds(pl.multiple_of(part * width, width), width)
        values = [eight_ref[pl.ds(row, 1), place] for row in range(8)] + [one_ref[:, place]]
        scatter_columns(values, column_ref[:, place], rows, total)

    entries = load_entries(params_ref, scr, rows)
    pulls = [total[pl.ds(quantity * rows, rows), :] for quantity in range(QUANT)]
    size = jnp.abs(pulls[0])
    for pull in pulls[1:]:
        size = jnp.maximum(size, jnp.abs(pull))
    touched = size > 0.0
    _, pullback = jax.vjp(lambda values: project(values, yaw_ref[0], yaw_ref[1]), entries)
    (gradients,) = pullback(pulls)
    for row in range(NPAR):
        scr[pl.ds(row * rows, rows), :] = jnp.where(touched, gradients[row], 0.0)
    extra = jnp.sum(scr[pl.ds(chunks, NPAR, stride=rows), :], axis=1, keepdims=True)
    lane = lax.broadcasted_iota(jnp.int32, (NPAR, LANES), 1)
    row_index = lax.broadcasted_iota(jnp.int32, (NPAR, LANES), 0)
    rates = jnp.where(row_index < 14, 0.0025, 0.000125)
    rates = jnp.where(row_index < 11, 0.05, rates)
    rates = jnp.where(row_index < 10, 0.001, rates)
    rates = jnp.where(row_index < 6, 0.005, rates)
    rates = jnp.where(row_index < 3, 0.00016, rates)
    fix_one = 1.0 - beta_one**ADAM_STEP
    fix_two = 1.0 - beta_two**ADAM_STEP
    for copy in moments_in:
        copy.wait()
    for chunk in range(chunks):
        place = slice(chunk * LANES, (chunk + 1) * LANES)
        gradient = scr[pl.ds(chunk, NPAR, stride=rows), :]
        if chunk == 0:
            gradient = gradient + jnp.where(lane == 0, extra, 0.0)
        moment = beta_one * first_ref[:, place] + (1.0 - beta_one) * gradient
        variance = beta_two * second_ref[:, place] + (1.0 - beta_two) * gradient * gradient
        change = rates * (moment / fix_one) / (jnp.sqrt(variance / fix_two) + adam_eps)
        new_params_ref[:, place] = params_ref[:, place] - change
        new_first_ref[:, place] = moment
        new_second_ref[:, place] = variance


def exchange(arrays, owners):
    counts = [each.shape[0] for each in arrays]
    values = jnp.concatenate(arrays, axis=0)
    sent = values.reshape(values.shape[0], owners, -1)
    got = lax.all_to_all(sent, ("owner", "render"), split_axis=1, concat_axis=1, tiled=True)
    got = got.reshape(values.shape)
    return [got[sum(counts[:item]) : sum(counts[: item + 1])] for item in range(len(arrays))]


def body(
    params, first_moment, second_moment, target, view_yaw, tile_ids, visible, tile_slots, depth_rank
):
    render = lax.axis_size("render")
    owners = lax.axis_size("owner") * render
    cap = visible.shape[2]
    slots = owners * cap
    held = params.shape[1]
    tiles, length = tile_slots.shape
    chunks = held // LANES
    rows = (chunks + 1 + 7) // 8 * 8
    f32 = jnp.float32
    vmem = pl.BlockSpec(memory_space=pltpu.VMEM)
    fused = cap % LANES == 0
    smem = pl.BlockSpec(memory_space=pltpu.SMEM)
    shared = [
        jax.ShapeDtypeStruct((8, slots), f32),
        jax.ShapeDtypeStruct((1, slots), f32),
        jax.ShapeDtypeStruct((2, rows, LANES), f32),
    ]
    room = [pltpu.VMEM((NPAR * rows, LANES), f32), pltpu.VMEM((QUANT * rows, LANES), f32)]
    sends = [pltpu.VMEM((8, slots), f32), pltpu.VMEM((1, slots), f32)]
    sems = [pltpu.SemaphoreType.DMA((owners, 2))] * 2
    if fused:
        eight, one, yaws, column = pl.pallas_call(
            functools.partial(owner_exchange_kernel, owners, render, cap, rows),
            out_shape=shared + [jax.ShapeDtypeStruct((1, slots), jnp.int32)],
            in_specs=[vmem, vmem, smem, smem],
            out_specs=[vmem] * 4,
            scratch_shapes=room
            + [pltpu.VMEM((1, owners * (cap + LANES)), jnp.int32)] * 2
            + sends
            + sems
            + sems,
            compiler_params=pltpu.CompilerParams(
                vmem_limit_bytes=56 * 1024 * 1024, collective_id=0, has_side_effects=True
            ),
            name="owner_project",
        )(params, visible, view_yaw, tile_ids)
    else:
        trig = jnp.stack([jnp.cos(view_yaw), jnp.sin(view_yaw)])
        trig = jnp.pad(trig, ((0, 6), (0, LANES - view_yaw.shape[0])))
        view = jnp.full((owners, 1), tile_ids[0] // tiles_view, jnp.int32)
        requests = jnp.concatenate([visible[0], view], axis=1).reshape(1, -1)
        (wanted,) = exchange([requests], owners)
        wanted = wanted.reshape(owners, cap + 1)
        index = wanted[:, :cap]
        asker = jnp.arange(owners, dtype=jnp.int32)[:, None]
        column = jnp.where(index == 0, held + asker, index).reshape(1, slots)
        views = jnp.pad(wanted[:, cap], (0, LANES - owners)).reshape(1, LANES)
        eight, one, yaws = pl.pallas_call(
            functools.partial(owner_kernel, cap, rows),
            out_shape=shared,
            scratch_shapes=room,
            compiler_params=VMEM,
            name="owner_project",
        )(params, column, views, trig)
        eight, one = exchange([eight, one], owners)
    rendered, grad_eight, grad_one = pl.pallas_call(
        functools.partial(tile_kernel, owners if fused else 0, render),
        out_shape=[
            jax.ShapeDtypeStruct(target.shape, f32),
            jax.ShapeDtypeStruct((8, slots), f32),
            jax.ShapeDtypeStruct((1, slots), f32),
        ],
        in_specs=[vmem, vmem, vmem, vmem, smem, vmem],
        scratch_shapes=[
            pltpu.VMEM((QUANT * slots // LANES, LANES), f32),
            pltpu.VMEM((slots // LANES, LANES), f32),
        ]
        + [
            pltpu.VMEM((PIX, length), f32),
            pltpu.VMEM((PIX, length), f32),
            pltpu.VMEM((2 * PIX, length), jnp.bfloat16),
            pltpu.VMEM((2 * PIX, length), jnp.bfloat16),
        ]
        * (8 if tiles % 8 == 0 else 1)
        + (sends + sems if fused else []),
        compiler_params=pltpu.CompilerParams(
            vmem_limit_bytes=56 * 1024 * 1024, collective_id=1, has_side_effects=True
        )
        if fused
        else VMEM,
        name="tile_step",
    )(eight, one, tile_slots, depth_rank, tile_ids, target)
    if not fused:
        grad_eight, grad_one = exchange([grad_eight, grad_one], owners)
    hbm = pl.BlockSpec(memory_space=pl.ANY)
    new_params, new_first, new_second = pl.pallas_call(
        functools.partial(update_kernel, rows),
        out_shape=[jax.ShapeDtypeStruct(params.shape, f32)] * 3,
        in_specs=[vmem, hbm, hbm, vmem, vmem, vmem, vmem],
        scratch_shapes=room
        + [
            pltpu.VMEM(params.shape, f32),
            pltpu.VMEM(params.shape, f32),
            pltpu.SemaphoreType.DMA((2,)),
        ],
        compiler_params=VMEM,
        name="adam_step",
    )(params, first_moment, second_moment, column, yaws, grad_eight, grad_one)
    return (new_params, new_first, new_second, rendered)


def solution(mesh):
    in_specs = (
        P(None, ("groups", "owner", "render")),
        P(None, ("groups", "owner", "render")),
        P(None, ("groups", "owner", "render")),
        P(None, ("groups", "owner", "render"), None),
        P("groups"),
        P(("groups", "owner", "render")),
        P(("groups", "owner", "render"), None, None),
        P(("groups", "owner", "render"), None),
        P(("groups", "owner", "render"), None),
    )
    out_specs = (
        P(None, ("groups", "owner", "render")),
        P(None, ("groups", "owner", "render")),
        P(None, ("groups", "owner", "render")),
        P(None, ("groups", "owner", "render"), None),
    )
    return jax.shard_map(body, mesh=mesh, in_specs=in_specs, out_specs=out_specs, check_vma=False)
```
